128 devices in a mesh: group: 8 (over y_hi, x), slab: 16 (over z, y_lo, core).
Axes of the slice: x: 4, y: 4 (y_hi: 2, y_lo: 2; y = y_hi * 2 + y_lo), z: 4, core: 2. Of those that a mesh axis runs over, the one named last changes fastest.
Arguments:
- velocity: float32 [3, 128, 128, 2048], P(None, None, None, ('group', 'slab')), may hold values from -30 to 30
- register: float32 [3, 128, 128, 2048], P(None, None, None, ('group', 'slab')), may hold values from -4 to 4
- past: float32 [7, 512, 32, 96], P(None, ('group', 'slab')), may hold values from -4 to 4
- basis: float32 [16, 8, 256, 12288], P('slab', 'group'), may hold values from -6 to 6
- owner: int32 [16, 8], replicated, may hold values from 0 to 7, each once within a row
Outputs:
- new_velocity: float32 [3, 128, 128, 2048], P(None, None, None, ('group', 'slab'))
- new_register: float32 [3, 128, 128, 2048], P(None, None, None, ('group', 'slab'))
- coeffs: float32 [256, 8], replicated
- factor: float32 [8, 8], replicated
- directions: float32 [16, 8, 8, 12288], P('slab', 'group')
The draws below stay inside these ranges and needn't reach their ends.
Inputs may be any that keep to these rules, and one draw needn't show every extreme that they name: Each row of owner names every group once.
All inputs are finite; a program needn't handle non-finite values.
Results may differ from the reference program's by a relative error of at most 0.000075.
Values sent between devices are 32-bit elements; how exact they have to be, the bound alone decides.
A program may use at most 256 MiB of HBM per device.

```python
import jax
import jax.numpy as jnp
from jax import lax

NX = 128
NY = 128
RANK = 256
PAST = 7
NZ = 2048
NXC = 32
NYC = 32
NZC = 512
ZCD = 4
XPL = 4
ROWS_BLK = 12288
N_GROUP = 8
N_SLAB = 16


def draw_velocity(key, part):
    key = jax.random.fold_in(key, 11)
    base_key, row_key = jax.random.split(key)
    xpos = jnp.arange(NX, dtype=jnp.float32) / NX
    zpos = jnp.arange(NZ, dtype=jnp.float32) / NZ
    ramp = jnp.exp(0.5 * jnp.log(3.0) * (xpos[:, None] + zpos[None, :]))
    levels = jax.random.uniform(row_key, (NY,), minval=jnp.log(0.5), maxval=jnp.log(2.0))
    scale = 0.7 * ramp[:, None, :] * jnp.exp(levels)[None, :, None]
    base = jax.random.normal(base_key, (3, NX, NY, NZ))
    return jnp.clip(base * scale[None], -30.0, 30.0).astype(jnp.float32)


def block_levels(stream_key, shape, shards, least, largest):
    factor_of, own = 1.0, jax.random.fold_in(stream_key, 6)
    for position, blocks in shards:
        steps = jnp.exp(jax.random.uniform(jax.random.fold_in(own, position), (blocks,), jnp.float32, least / len(shards), largest / len(shards)))
        factor_of = factor_of * jnp.repeat(steps, shape[position] // blocks).reshape([-1 if axis == position else 1 for axis in range(len(shape))])
    return factor_of


def noise(stream_key, extent, spread, bound, pieces=(), kind=jnp.bfloat16):
    gain = block_levels(stream_key, extent, pieces, -0.22, 0.18) if pieces else 1.0
    values = jax.random.normal(stream_key, extent, jnp.float32) * spread * gain
    return jnp.minimum(jnp.maximum(values, -bound), bound).astype(kind)


def setup_inputs(seed: int = 0) -> dict:
    key_of = jax.random.split(jax.random.key(seed), 6)
    velocity = draw_velocity(jax.random.fold_in(key_of[5], 71), 0)
    register = noise(key_of[1], (3, NX, NY, NZ), 0.3, 4.0, ((3, 128),), jnp.float32)
    past = noise(key_of[2], (PAST, NZC, NXC, 3 * NYC), 0.25, 4.0, ((1, 128),), jnp.float32)
    basis = noise(key_of[3], (N_SLAB, N_GROUP, RANK, ROWS_BLK), 1.0, 6.0, ((0, 16), (1, 8)), jnp.float32)
    owner = jax.vmap(lambda own: jax.random.permutation(own, N_GROUP))(jax.random.split(key_of[4], N_SLAB)).reshape((N_SLAB, N_GROUP)).astype(jnp.int32)
    return dict(velocity=velocity, register=register, past=past, basis=basis, owner=owner)


first_coef = (0.8, -0.2, 4.0 / 105.0, -1.0 / 280.0)
second_coef = (-205.0 / 72.0, 1.6, -0.2, 8.0 / 315.0, -1.0 / 560.0)
time_step = 0.02
viscosity = 0.4
section_decay = -5.0 / 9.0
section_gain = 15.0 / 16.0

def difference(shifted, center):
    first = first_coef[0] * (shifted(1) - shifted(-1))
    for offset in range(2, 5):
        first = first + first_coef[offset - 1] * (shifted(offset) - shifted(-offset))
    second = second_coef[0] * center
    for offset in range(1, 5):
        second = second + second_coef[offset] * (shifted(offset) + shifted(-offset))
    return (first, second)

def axis_term(velocity, component, shifted):
    first, second = difference(shifted, velocity)
    return viscosity * second - velocity[component][None] * first

def coarsen(field):
    comps, wide_x, wide_y, wide_z = field.shape
    boxes = field.reshape(comps, wide_x // 4, 4, wide_y // 4, 4, wide_z // 4, 4).mean(axis=(2, 4, 6))
    return boxes.transpose(3, 1, 0, 2).reshape(wide_z // 4, wide_x // 4, comps * (wide_y // 4))

def tri_solve(lower_mat, rhs, transposed):
    return lax.linalg.triangular_solve(lower_mat, rhs, left_side=True, lower=True, transpose_a=transposed)

def reference(velocity, register, past, basis, owner):

    def roller(axis):
        return lambda offset: jnp.roll(velocity, -offset, axis=axis)
    term_x = axis_term(velocity, 0, roller(1))
    term_y = axis_term(velocity, 1, roller(2))
    term_z = axis_term(velocity, 2, roller(3))
    tendency = term_x + term_y + term_z
    new_register = section_decay * register + time_step * tendency
    new_velocity = velocity + section_gain * new_register
    fresh = coarsen(new_velocity)[None]
    snaps = jnp.concatenate([past, fresh], axis=0)
    count = snaps.shape[0]
    blocks = snaps.reshape(count, N_GROUP, N_SLAB, ZCD, N_GROUP, XPL, 3 * NYC).transpose(2, 4, 0, 3, 1, 5, 6)
    inverse = jnp.argsort(owner, axis=1).astype(jnp.int32)
    picked = jnp.take_along_axis(blocks, inverse[:, :, None, None, None, None, None], axis=1)
    rows = picked.reshape(N_SLAB, N_GROUP, count, ROWS_BLK)
    total = float(ROWS_BLK * N_SLAB * N_GROUP)
    high = lax.Precision.HIGHEST
    proj = jnp.einsum('sgrn,sgtn->rt', basis, rows, precision=high) / total
    gram = jnp.einsum('sgrn,sgqn->rq', basis, basis, precision=high) / total
    chol = jnp.linalg.cholesky(gram)
    coeffs = tri_solve(chol, tri_solve(chol, proj, False), True)
    residual = rows - jnp.einsum('sgrn,rt->sgtn', basis, coeffs, precision=high)
    wgram = jnp.einsum('sgtn,sgun->tu', residual, residual, precision=high) / total
    factor = jnp.linalg.cholesky(wgram)
    flat = residual.transpose(2, 0, 1, 3).reshape(count, -1)
    solved = tri_solve(factor, flat, False)
    directions = solved.reshape(count, N_SLAB, N_GROUP, ROWS_BLK).transpose(1, 2, 0, 3)
    return (new_velocity, new_register, coeffs, factor, directions)
```

```python
import functools

import jax
import jax.numpy as jnp
from jax import lax
from jax.experimental import pallas as pl
from jax.experimental.pallas import tpu as pltpu
from jax.sharding import PartitionSpec as P

first_coef = (0.8, -0.2, 4.0 / 105.0, -1.0 / 280.0)
second_coef = (-205.0 / 72.0, 1.6, -0.2, 8.0 / 315.0, -1.0 / 560.0)
time_step = 0.02
viscosity = 0.4
section_decay = -5.0 / 9.0
section_gain = 15.0 / 16.0
reach = 4

F32 = jnp.float32
BF16 = jnp.bfloat16
HIGH = lax.Precision.HIGHEST
NT = (((1,), (1,)), ((), ()))
TN = (((0,), (0,)), ((), ()))
NN = (((1,), (0,)), ((), ()))
N_GROUP = 8
N_SLAB = 16
RANK = 256
ROWS = 12288
COUNT = 8
PLANES = 4
LANES = 384
CHUNK = 1024
N_CHUNK = ROWS // CHUNK
BAND = RANK // N_SLAB
MIB = 2**20


def dot(left, right, dims, precision=None):
    return lax.dot_general(
        left, right, dims, precision=precision, preferred_element_type=F32
    )


def split(value):
    high = value.astype(BF16)
    return high, (value - high.astype(F32)).astype(BF16)


def peer(axis, step):
    group, slab = lax.axis_index("group"), lax.axis_index("slab")
    if axis == "group":
        return (lax.rem(group + step, N_GROUP), slab)
    return (group, lax.rem(slab + step, N_SLAB))


def linear(step):
    total = N_GROUP * N_SLAB
    place = lax.rem(lax.axis_index("group") * N_SLAB + lax.axis_index("slab") + step + total, total)
    return (place // N_SLAB, lax.rem(place, N_SLAB))


def greet(halo):
    barrier = pltpu.get_barrier_semaphore()
    count = 0
    for axis, size in (("group", N_GROUP), ("slab", N_SLAB)):

        def hello(step, carry, axis=axis):
            pl.semaphore_signal(barrier, inc=1, device_id=peer(axis, step))
            return carry

        lax.fori_loop(1, size, hello, 0)
        count += size - 1
    if halo:
        for step in (1, -1):
            pl.semaphore_signal(barrier, inc=1, device_id=linear(step))
            count += 1
    pl.semaphore_wait(barrier, count)


def broadcast(axis, size, source, target, send_sem, recv_sem):
    def send(step, carry):
        pltpu.make_async_remote_copy(
            src_ref=source(step),
            dst_ref=target,
            send_sem=send_sem,
            recv_sem=recv_sem,
            device_id=peer(axis, step),
        ).start()
        return carry

    lax.fori_loop(1, size, send, 0)


def drain(ref, *sems):
    for sem in sems:
        pltpu.make_async_copy(ref, ref, sem).wait()


def add_slots(ref):
    total = ref[0]
    for slot in range(1, ref.shape[0]):
        total = total + ref[slot]
    return total


def piece_of(owner, group):
    slab = lax.axis_index("slab")
    place = jnp.int32(0)
    for piece in range(N_GROUP):
        place = jnp.where(owner[slab, piece] == group, piece, place)
    return place


def front_kernel(
    velocity, basis, past, owner,
    low, high, gram, rows,
    field, edge_low, edge_high, blocks, past_v, pieces, ship, local, shares, partial, groups, band, full,
    field_sem, halo_send, halo_recv, block_sem, past_sem, piece_send, piece_recv, own_sem, sum_send, sum_recv, out_sem,
):
    group, slab = lax.axis_index("group"), lax.axis_index("slab")
    loads = [
        pltpu.make_async_copy(velocity.at[c], field.at[c], field_sem.at[c]) for c in range(3)
    ]
    for load in loads:
        load.start()
    past_load = pltpu.make_async_copy(past, past_v, past_sem)
    past_load.start()

    def block_load(step):
        lanes = pl.ds(pl.multiple_of(step * CHUNK, CHUNK), CHUNK)
        return pltpu.make_async_copy(basis.at[:, lanes], blocks.at[step], block_sem.at[step])

    def begin(step, carry):
        block_load(step).start()
        return carry

    lax.fori_loop(0, N_CHUNK, begin, 0)
    greet(True)

    halos = []
    for c in range(3):
        loads[c].wait()
        edge_low[c] = field[c, :, 0:reach, :]
        edge_high[c] = field[c, :, 16 - reach : 16, :]
        for side, (edge, target, step) in enumerate(((edge_high, low, 1), (edge_low, high, -1))):
            copy = pltpu.make_async_remote_copy(
                src_ref=edge.at[c],
                dst_ref=target.at[c],
                send_sem=halo_send.at[side, c],
                recv_sem=halo_recv.at[side, c],
                device_id=linear(step),
            )
            copy.start()
            halos.append(copy)

    past_load.wait()
    pieces[...] = jnp.zeros_like(pieces)

    def arrange(place, carry):
        piece, plane = place // PLANES, lax.rem(place, PLANES)
        parts = [past_v[:, plane, pl.ds(piece * 4 + j, 1), :].reshape(COUNT - 1, 96) for j in range(4)]
        pieces[piece, plane, 0 : COUNT - 1, :] = jnp.concatenate(parts, axis=1)
        return carry

    lax.fori_loop(0, N_GROUP * PLANES, arrange, 0)

    def pick(step, carry):
        ship[step] = pieces[piece_of(owner, lax.rem(group + step, N_GROUP))]
        return carry

    lax.fori_loop(0, N_GROUP, pick, 0)
    own = pltpu.make_async_copy(ship.at[0], rows.at[:, group], own_sem)
    own.start()
    broadcast("group", N_GROUP, lambda step: ship.at[step], rows.at[:, group], piece_send, piece_recv)

    local[...] = jnp.zeros_like(local)

    def multiply(step, carry):
        block_load(step).wait()
        top, rest = split(blocks[step])
        local[...] += dot(top, jnp.concatenate([top, rest], axis=0), NT)
        return carry

    lax.fori_loop(0, N_CHUNK, multiply, 0)
    cross = local[:, RANK:]
    partial[...] = (local[:, :RANK] + cross + cross.T).reshape(N_SLAB, BAND, RANK)

    broadcast(
        "slab", N_SLAB, lambda step: partial.at[lax.rem(slab + step, N_SLAB)], shares.at[slab],
        sum_send.at[0], sum_recv.at[0],
    )
    shares[slab] = partial[slab]
    drain(shares.at[pl.ds(0, N_SLAB - 1)], sum_recv.at[0], sum_send.at[0])
    groups[group] = add_slots(shares)
    broadcast(
        "group", N_GROUP, lambda step: groups.at[group], groups.at[group], sum_send.at[1], sum_recv.at[1]
    )
    drain(groups.at[pl.ds(0, N_GROUP - 1)], sum_recv.at[1], sum_send.at[1])
    band[...] = add_slots(groups) * (1.0 / (ROWS * N_GROUP * N_SLAB))
    full[slab] = band[...]
    broadcast("slab", N_SLAB, lambda step: band, full.at[slab], sum_send.at[2], sum_recv.at[2])
    drain(full.at[pl.ds(0, N_SLAB - 1)], sum_recv.at[2], sum_send.at[2])
    out = pltpu.make_async_copy(full, gram, out_sem)
    out.start()

    own.wait()
    drain(ship.at[pl.ds(0, N_GROUP - 1)], piece_recv, piece_send)
    for copy in halos:
        copy.wait()
    out.wait()


def front(velocity, basis, past, owner):
    any_space = pl.BlockSpec(memory_space=pl.ANY)
    return pl.pallas_call(
        front_kernel,
        in_specs=[any_space] * 3 + [pl.BlockSpec(memory_space=pltpu.SMEM)],
        out_specs=[any_space] * 4,
        out_shape=[
            jax.ShapeDtypeStruct((3, 128, reach, 128), F32),
            jax.ShapeDtypeStruct((3, 128, reach, 128), F32),
            jax.ShapeDtypeStruct((N_SLAB, BAND, RANK), F32),
            jax.ShapeDtypeStruct((PLANES, N_GROUP, COUNT, LANES), F32),
        ],
        scratch_shapes=[
            pltpu.VMEM((3, 128, 16, 128), F32),
            pltpu.VMEM((3, 128, reach, 128), F32),
            pltpu.VMEM((3, 128, reach, 128), F32),
            pltpu.VMEM((N_CHUNK, RANK, CHUNK), F32),
            pltpu.VMEM((COUNT - 1, PLANES, 32, 96), F32),
            pltpu.VMEM((N_GROUP, PLANES, COUNT, LANES), F32),
            pltpu.VMEM((N_GROUP, PLANES, COUNT, LANES), F32),
            pltpu.VMEM((RANK, 2 * RANK), F32),
            pltpu.VMEM((N_SLAB, BAND, RANK), F32),
            pltpu.VMEM((N_SLAB, BAND, RANK), F32),
            pltpu.VMEM((N_GROUP, BAND, RANK), F32),
            pltpu.VMEM((BAND, RANK), F32),
            pltpu.VMEM((N_SLAB, BAND, RANK), F32),
            pltpu.SemaphoreType.DMA((3,)),
            pltpu.SemaphoreType.DMA((2, 3)),
            pltpu.SemaphoreType.DMA((2, 3)),
            pltpu.SemaphoreType.DMA((N_CHUNK,)),
            pltpu.SemaphoreType.DMA,
            pltpu.SemaphoreType.DMA,
            pltpu.SemaphoreType.DMA,
            pltpu.SemaphoreType.DMA,
            pltpu.SemaphoreType.DMA((3,)),
            pltpu.SemaphoreType.DMA((3,)),
            pltpu.SemaphoreType.DMA,
        ],
        compiler_params=pltpu.CompilerParams(
            collective_id=0, has_side_effects=True, vmem_limit_bytes=56 * MIB
        ),
        name="front",
    )(velocity, basis, past, owner)


X_BLOCK = 16


def stencil_kernel(v, low, high, register, new_v, new_r, fresh, sums_ref):
    block = pl.program_id(0)

    def column(within):
        x = block * X_BLOCK + within
        center = [v[c, x] for c in range(3)]
        coef = []
        for axis in range(3):
            row = []
            for k in range(4):
                drift = center[axis] * first_coef[k]
                diffuse = viscosity * second_coef[k + 1]
                row.append((diffuse - drift, diffuse + drift))
            coef.append(row)
        outs = []
        for c in range(3):
            tall = jnp.concatenate([low[c, x], center[c], high[c, x]], axis=0)
            total = center[c] * (3.0 * viscosity * second_coef[0])
            for k in range(1, 5):
                up, down = coef[0][k - 1]
                total = total + v[c, (x + k) & 127] * up + v[c, (x - k) & 127] * down
            for k in range(1, 5):
                up, down = coef[1][k - 1]
                total = total + pltpu.roll(center[c], 128 - k, 1) * up
                total = total + pltpu.roll(center[c], k, 1) * down
            for k in range(1, 5):
                up, down = coef[2][k - 1]
                total = total + tall[reach + k : reach + k + 16] * up
                total = total + tall[reach - k : reach - k + 16] * down
            moved = register[c, within] * section_decay + time_step * total
            new_r[c, within] = moved
            fluid = center[c] + section_gain * moved
            new_v[c, within] = fluid
            outs.append(fluid)
        return outs

    def coarse(quad, carry):
        sums = column(quad * 4)
        for j in range(1, 4):
            sums = [a + b for a, b in zip(sums, column(quad * 4 + j))]
        across = block * (X_BLOCK // 4) + quad
        j, piece = across & 3, across >> 2
        for c in range(3):
            place = ((c * 4 + j) * N_GROUP + piece) * 16
            sums_ref[pl.ds(pl.multiple_of(place, 16), 16), :] = sums[c]
        return carry

    lax.fori_loop(0, X_BLOCK // 4, coarse, 0)

    @pl.when(block == pl.num_programs(0) - 1)
    def _():
        rows = sums_ref[pl.ds(0, 384, 4), :]
        for z in range(1, 4):
            rows = rows + sums_ref[pl.ds(z, 384, 4), :]
        row = lax.broadcasted_iota(jnp.int32, (512, 128), 0)
        lane = lax.broadcasted_iota(jnp.int32, (512, 128), 1)
        fold = jnp.where((row // 128 == lane // 32) & ((row % 128) // 4 == lane % 32), 1 / 64, 0.0)
        for tile in range(3):
            parts = []
            for m in range(4):
                j, c = divmod(4 * tile + m, 3)
                parts.append(rows[(c * 4 + j) * 32 : (c * 4 + j) * 32 + 32])
            fresh[:, tile * 128 : (tile + 1) * 128] = dot(
                jnp.concatenate(parts, axis=1), fold.astype(F32), NN, HIGH
            )


def stencil(velocity, low, high, register):
    vmem = pl.BlockSpec(memory_space=pltpu.VMEM)
    part = pl.BlockSpec((3, X_BLOCK, 16, 128), lambda i: (0, i, 0, 0))
    return pl.pallas_call(
        stencil_kernel,
        grid=(128 // X_BLOCK,),
        in_specs=[vmem, vmem, vmem, part],
        out_specs=[part, part, pl.BlockSpec((32, LANES), lambda i: (0, 0))],
        out_shape=[
            jax.ShapeDtypeStruct((3, 128, 16, 128), F32),
            jax.ShapeDtypeStruct((3, 128, 16, 128), F32),
            jax.ShapeDtypeStruct((32, LANES), F32),
        ],
        scratch_shapes=[pltpu.VMEM((1536, 128), F32)],
        compiler_params=pltpu.CompilerParams(vmem_limit_bytes=50 * MIB),
        name="stencil",
    )(velocity, low, high, register)


def sweep_block(block):
    size = block.shape[0]
    lane = lax.broadcasted_iota(jnp.int32, block.shape, 1)
    row = lax.broadcasted_iota(jnp.int32, block.shape, 0)
    for q in range(size):
        pivot = 1.0 / block[q : q + 1, q : q + 1]
        line = jnp.where(lane[:1] == q, -1.0, block[q : q + 1, :]) * pivot
        column = block[:, q : q + 1]
        block = jnp.where(lane == q, 0.0, block) - column * line
        block = jnp.where(row == q, line, block)
    return -block


BLOCK = 32


def invert(matrix):
    lane = lax.broadcasted_iota(jnp.int32, (BLOCK, RANK), 1)
    row = lax.broadcasted_iota(jnp.int32, (BLOCK, RANK), 0)
    wide = lax.broadcasted_iota(jnp.int32, (RANK, RANK), 1)
    for k in range(RANK // BLOCK):
        start = k * BLOCK
        panel = matrix[start : start + BLOCK, :]
        tile = start // 128 * 128
        diagonal = panel[:, tile : tile + 128]
        if start % 128:
            diagonal = pltpu.roll(diagonal, 128 - start % 128, 1)
        inverse = sweep_block(diagonal)[:, :BLOCK]
        inside = (lane >= start) & (lane < start + BLOCK)
        eye = jnp.where(lane - start == row, -1.0, 0.0)
        solved = dot(inverse, jnp.where(inside, eye, panel), NN, HIGH)
        inside = (wide >= start) & (wide < start + BLOCK)
        matrix[...] = jnp.where(inside, 0.0, matrix[...]) - dot(panel, solved, TN, HIGH)
        matrix[start : start + BLOCK, :] = solved


def back_kernel(
    rows, gram, basis, fresh, owner,
    coeffs, factor, directions,
    blocks, top, rest, rows_v, fresh_v, ship, pieces, sheet, matrix, proj_group, proj_slab, res_group, res_slab,
    block_sem, rows_sem, gram_sem, fresh_sem, piece_send, piece_recv, sum_send, sum_recv,
):
    group, slab = lax.axis_index("group"), lax.axis_index("slab")
    fresh_load = pltpu.make_async_copy(fresh, fresh_v, fresh_sem)
    fresh_load.start()
    gram_load = pltpu.make_async_copy(gram, matrix, gram_sem)
    gram_load.start()
    rows_load = pltpu.make_async_copy(rows, rows_v, rows_sem)
    rows_load.start()

    def block_load(step):
        lanes = pl.ds(pl.multiple_of(step * CHUNK, CHUNK), CHUNK)
        return pltpu.make_async_copy(basis.at[:, lanes], blocks.at[step], block_sem.at[step])

    def begin(step, carry):
        block_load(step).start()
        return carry

    lax.fori_loop(0, N_CHUNK, begin, 0)
    greet(False)
    fresh_load.wait()

    def pick(step, carry):
        ship[step] = fresh_v[piece_of(owner, lax.rem(group + step, N_GROUP))]
        return carry

    lax.fori_loop(0, N_GROUP, pick, 0)
    pieces[group] = ship[0]
    broadcast("group", N_GROUP, lambda step: ship.at[step], pieces.at[group], piece_send, piece_recv)

    gram_load.wait()
    invert(matrix)

    rows_load.wait()
    drain(pieces.at[pl.ds(0, N_GROUP - 1)], piece_recv, piece_send)
    last = lax.broadcasted_iota(jnp.int32, (COUNT, LANES), 0) == COUNT - 1
    for plane in range(PLANES):
        for h in range(N_GROUP):
            start = (plane * N_GROUP + h) * LANES
            sheet[:, start : start + LANES] = jnp.where(
                last, pieces[h, plane : plane + 1, :], rows_v[plane, h]
            )

    def lanes_of(step):
        return pl.ds(pl.multiple_of(step * CHUNK, CHUNK), CHUNK)

    def project(step, total):
        block_load(step).wait()
        upper, lower = split(blocks[step])
        top[step], rest[step] = upper, lower
        part = sheet[:, lanes_of(step)]
        head, tail = split(part)
        both = dot(jnp.concatenate([head, tail], axis=0), upper, NT)
        return total + both[:COUNT] + both[COUNT:] + dot(head, lower, NT)

    proj = lax.fori_loop(0, N_CHUNK, project, jnp.zeros((COUNT, RANK), F32))

    def sum_all(value, group_ref, slab_ref, place):
        group_ref[group] = value
        broadcast(
            "group", N_GROUP, lambda step: group_ref.at[group], group_ref.at[group],
            sum_send.at[place], sum_recv.at[place],
        )
        drain(group_ref.at[pl.ds(0, N_GROUP - 1)], sum_recv.at[place], sum_send.at[place])
        slab_ref[slab] = add_slots(group_ref)
        broadcast(
            "slab", N_SLAB, lambda step: slab_ref.at[slab], slab_ref.at[slab],
            sum_send.at[place + 1], sum_recv.at[place + 1],
        )
        drain(slab_ref.at[pl.ds(0, N_SLAB - 1)], sum_recv.at[place + 1], sum_send.at[place + 1])
        return add_slots(slab_ref) * (1.0 / (ROWS * N_GROUP * N_SLAB))

    proj = sum_all(proj, proj_group, proj_slab, 0)
    weights = -dot(proj, matrix[...], NN, HIGH)
    coeffs[...] = weights

    head, tail = split(weights)
    both_parts = jnp.concatenate([head, tail], axis=0)

    def subtract(step, total):
        both = dot(both_parts, top[step], NN)
        image = both[:COUNT] + both[COUNT:] + dot(head, rest[step], NN)
        part = sheet[:, lanes_of(step)] - image
        sheet[:, lanes_of(step)] = part
        return total + dot(part, part, NT, HIGH)

    wgram = lax.fori_loop(0, N_CHUNK, subtract, jnp.zeros((COUNT, COUNT), F32))
    wgram = jnp.concatenate([wgram, jnp.zeros((COUNT, 128 - COUNT), F32)], axis=1)
    wgram = sum_all(wgram, res_group, res_slab, 2)

    lane = lax.broadcasted_iota(jnp.int32, (COUNT, 128), 1)
    row = lax.broadcasted_iota(jnp.int32, (COUNT, 128), 0)
    lower = jnp.zeros((COUNT, 128), F32)
    inverse = jnp.where(lane == row, 1.0, 0.0)
    for q in range(COUNT):
        scale = lax.rsqrt(wgram[q : q + 1, q : q + 1])
        column = wgram[:, q : q + 1] * scale
        column = jnp.where(row[:, :1] >= q, column, 0.0)
        lower = jnp.where(lane == q, column, lower)
        line = wgram[q : q + 1, :] * scale
        below = jnp.where(row[:, :1] > q, column, 0.0)
        wgram = wgram - below * line
        solved = inverse[q : q + 1, :] * scale
        inverse = jnp.where(row == q, solved, inverse - below * solved)
    factor[...] = lower[:, :COUNT]
    columns = [inverse[:, q : q + 1] for q in range(COUNT)]

    def direct(step, carry):
        part = sheet[:, lanes_of(step)]
        total = columns[0] * part[0:1, :]
        for q in range(1, COUNT):
            total = total + columns[q] * part[q : q + 1, :]
        directions[:, lanes_of(step)] = total
        return carry

    lax.fori_loop(0, N_CHUNK, direct, 0)


def back(rows, gram, basis, fresh, owner):
    any_space = pl.BlockSpec(memory_space=pl.ANY)
    vmem = pl.BlockSpec(memory_space=pltpu.VMEM)
    return pl.pallas_call(
        back_kernel,
        in_specs=[any_space] * 4 + [pl.BlockSpec(memory_space=pltpu.SMEM)],
        out_specs=[vmem] * 3,
        out_shape=[
            jax.ShapeDtypeStruct((COUNT, RANK), F32),
            jax.ShapeDtypeStruct((COUNT, COUNT), F32),
            jax.ShapeDtypeStruct((COUNT, ROWS), F32),
        ],
        scratch_shapes=[
            pltpu.VMEM((N_CHUNK, RANK, CHUNK), F32),
            pltpu.VMEM((N_CHUNK, RANK, CHUNK), BF16),
            pltpu.VMEM((N_CHUNK, RANK, CHUNK), BF16),
            pltpu.VMEM((PLANES, N_GROUP, COUNT, LANES), F32),
            pltpu.VMEM((N_GROUP, PLANES, LANES), F32),
            pltpu.VMEM((N_GROUP, PLANES, LANES), F32),
            pltpu.VMEM((N_GROUP, PLANES, LANES), F32),
            pltpu.VMEM((COUNT, ROWS), F32),
            pltpu.VMEM((RANK, RANK), F32),
            pltpu.VMEM((N_GROUP, COUNT, RANK), F32),
            pltpu.VMEM((N_SLAB, COUNT, RANK), F32),
            pltpu.VMEM((N_GROUP, COUNT, 128), F32),
            pltpu.VMEM((N_SLAB, COUNT, 128), F32),
            pltpu.SemaphoreType.DMA((N_CHUNK,)),
            pltpu.SemaphoreType.DMA,
            pltpu.SemaphoreType.DMA,
            pltpu.SemaphoreType.DMA,
            pltpu.SemaphoreType.DMA,
            pltpu.SemaphoreType.DMA,
            pltpu.SemaphoreType.DMA((4,)),
            pltpu.SemaphoreType.DMA((4,)),
        ],
        compiler_params=pltpu.CompilerParams(
            collective_id=1, has_side_effects=True, vmem_limit_bytes=56 * MIB
        ),
        name="back",
    )(rows, gram, basis, fresh, owner)


def local(velocity, register, past, basis, owner):
    field = velocity.transpose(0, 1, 3, 2)
    blocks = basis.reshape(RANK, ROWS)
    low, high, gram, rows = front(field, blocks, past, owner)
    new_v, new_r, fresh = stencil(field, low, high, register.transpose(0, 1, 3, 2))
    coeffs, factor, directions = back(
        rows, gram.reshape(RANK, RANK), blocks, fresh.reshape(N_GROUP, PLANES, LANES), owner
    )
    return (
        new_v.transpose(0, 1, 3, 2),
        new_r.transpose(0, 1, 3, 2),
        coeffs.T,
        factor,
        directions.reshape(1, 1, COUNT, ROWS),
    )


def solution(mesh):
    in_specs = (
        P(None, None, None, ("group", "slab")),
        P(None, None, None, ("group", "slab")),
        P(None, ("group", "slab"), None, None),
        P("slab", "group", None, None),
        P(),
    )
    out_specs = (
        P(None, None, None, ("group", "slab")),
        P(None, None, None, ("group", "slab")),
        P(),
        P(),
        P("slab", "group", None, None),
    )
    return jax.shard_map(local, mesh=mesh, in_specs=in_specs, out_specs=out_specs, check_vma=False)
```

```python
import functools

import jax
import jax.numpy as jnp
from jax import lax
from jax.experimental import pallas as pl
from jax.experimental.pallas import tpu as pltpu
from jax.sharding import PartitionSpec as P

first_coef = (0.8, -0.2, 4.0 / 105.0, -1.0 / 280.0)
second_coef = (-205.0 / 72.0, 1.6, -0.2, 8.0 / 315.0, -1.0 / 560.0)
time_step = 0.02
viscosity = 0.4
section_decay = -5.0 / 9.0
section_gain = 15.0 / 16.0
reach = 4

F32 = jnp.float32
BF16 = jnp.bfloat16
HIGH = lax.Precision.HIGHEST
NT = (((1,), (1,)), ((), ()))
TN = (((0,), (0,)), ((), ()))
NN = (((1,), (0,)), ((), ()))
N_GROUP = 8
N_SLAB = 16
N_POLE = 8
N_PLANE = 16
RANK = 256
ROWS = 12288
COUNT = 8
PLANES = 4
LANES = 384
CHUNK = 1024
N_CHUNK = ROWS // CHUNK
BAND = RANK // N_SLAB
X_CHUNK = 16
N_X = 128 // X_CHUNK
BLOCK = 32
MIB = 2**20


def dot(left, right, dims, precision=None):
    return lax.dot_general(
        left, right, dims, precision=precision, preferred_element_type=F32
    )


def split(value):
    high = value.astype(BF16)
    return high, (value - high.astype(F32)).astype(BF16)


def peer(axis, step):
    group, slab = lax.axis_index("group"), lax.axis_index("slab")
    if axis == "group":
        return (lax.rem(group + step, N_GROUP), slab)
    if axis == "slab":
        return (group, lax.rem(slab + step, N_SLAB))
    column = lax.rem(slab // 2, 2)
    if axis == "pole":
        place = lax.rem(pole_index() + step, N_POLE)
        return (group, place // 2 * 4 + column * 2 + lax.rem(place, 2))
    place = lax.rem(plane_index() + step, N_PLANE)
    return (place // 2, slab - column * 2 + lax.rem(place, 2) * 2)


def pole_index():
    slab = lax.axis_index("slab")
    return slab // 4 * 2 + lax.rem(slab, 2)


def plane_index():
    return lax.axis_index("group") * 2 + lax.rem(lax.axis_index("slab") // 2, 2)


def linear(step):
    total = N_GROUP * N_SLAB
    place = lax.rem(lax.axis_index("group") * N_SLAB + lax.axis_index("slab") + step + total, total)
    return (place // N_SLAB, lax.rem(place, N_SLAB))


def hello():
    barrier = pltpu.get_barrier_semaphore()
    for axis, size in (("slab", N_SLAB), ("plane", N_PLANE)):

        def signal(step, carry, axis=axis):
            pl.semaphore_signal(barrier, inc=1, device_id=peer(axis, step))
            return carry

        lax.fori_loop(1, size, signal, 0)
    for step in (1, -1):
        pl.semaphore_signal(barrier, inc=1, device_id=linear(step))


def everyone_in():
    pl.semaphore_wait(pltpu.get_barrier_semaphore(), N_SLAB + N_PLANE)


def broadcast(axis, size, source, target, send_sem, recv_sem):
    def send(step, carry):
        pltpu.make_async_remote_copy(
            src_ref=source(step),
            dst_ref=target,
            send_sem=send_sem,
            recv_sem=recv_sem,
            device_id=peer(axis, step),
        ).start()
        return carry

    lax.fori_loop(1, size, send, 0)


def drain(ref, *sems):
    for sem in sems:
        pltpu.make_async_copy(ref, ref, sem).wait()


def add_slots(ref):
    total = ref[0]
    for slot in range(1, ref.shape[0]):
        total = total + ref[slot]
    return total


def piece_of(owner, group):
    slab = lax.axis_index("slab")
    place = jnp.int32(0)
    for piece in range(N_GROUP):
        place = jnp.where(owner[piece, slab] == group, piece, place)
    return place


def sweep_block(block):
    lane = lax.broadcasted_iota(jnp.int32, (8, 128), 1)
    row = lax.broadcasted_iota(jnp.int32, (8, 128), 0)
    count = block.shape[0] // 8
    parts = [block[8 * i : 8 * i + 8] for i in range(count)]
    for b in range(count):
        line = parts[b]
        columns = [jnp.broadcast_to(line[:, 8 * b + j : 8 * b + j + 1], (8, 128)) for j in range(8)]
        inside = (lane >= 8 * b) & (lane < 8 * b + 8)
        line = jnp.where(inside, jnp.where(lane - 8 * b == row, -1.0, 0.0), line)
        for q in range(8):
            pivot = 1.0 / columns[q][q : q + 1, :]
            solved = line[q : q + 1, :] * pivot
            others = jnp.where(row == q, 0.0, columns[q])
            line = jnp.where(row == q, solved, line - others * solved)
            for j in range(q + 1, 8):
                entry = columns[j][q : q + 1, :] * pivot
                columns[j] = jnp.where(row == q, entry, columns[j] - others * entry)
        for i in range(count):
            if i != b:
                part = parts[i]
                total = jnp.where(inside, 0.0, part)
                for j in range(8):
                    column = jnp.broadcast_to(part[:, 8 * b + j : 8 * b + j + 1], (8, 128))
                    total = total - column * line[j : j + 1, :]
                parts[i] = total
        parts[b] = line
    return -jnp.concatenate(parts, axis=0)


def invert(matrix, first, last):
    lane = lax.broadcasted_iota(jnp.int32, (BLOCK, RANK), 1)
    row = lax.broadcasted_iota(jnp.int32, (BLOCK, RANK), 0)
    wide = lax.broadcasted_iota(jnp.int32, (RANK, RANK), 1)
    for k in range(first, last):
        start = k * BLOCK
        panel = matrix[start : start + BLOCK, :]
        tile = start // 128 * 128
        diagonal = panel[:, tile : tile + 128]
        if start % 128:
            diagonal = pltpu.roll(diagonal, 128 - start % 128, 1)
        inverse = sweep_block(diagonal)[:, :BLOCK]
        inside = (lane >= start) & (lane < start + BLOCK)
        eye = jnp.where(lane - start == row, -1.0, 0.0)
        solved = dot(inverse, jnp.where(inside, eye, panel), NN, HIGH)
        inside = (wide >= start) & (wide < start + BLOCK)
        matrix[...] = jnp.where(inside, 0.0, matrix[...]) - dot(panel, solved, TN, HIGH)
        matrix[start : start + BLOCK, :] = solved


def fold_fresh(sums_ref, fresh):
    rows = sums_ref[pl.ds(0, 384, 4), :]
    for z in range(1, 4):
        rows = rows + sums_ref[pl.ds(z, 384, 4), :]
    row = lax.broadcasted_iota(jnp.int32, (512, 128), 0)
    lane = lax.broadcasted_iota(jnp.int32, (512, 128), 1)
    fold = jnp.where((row // 128 == lane // 32) & ((row % 128) // 4 == lane % 32), 1 / 64, 0.0)
    for tile in range(3):
        parts = []
        for m in range(4):
            j, c = divmod(4 * tile + m, 3)
            parts.append(rows[(c * 4 + j) * 32 : (c * 4 + j) * 32 + 32])
        part = dot(jnp.concatenate(parts, axis=1), fold.astype(F32), NN, HIGH)
        fresh[:, :, tile * 128 : (tile + 1) * 128] = part.reshape(N_GROUP, PLANES, 128)


def column(v, low, high, register, new_v, x):
    center = [v[c, x] for c in range(3)]
    coef = []
    for axis in range(3):
        row = []
        for k in range(4):
            drift = center[axis] * first_coef[k]
            diffuse = viscosity * second_coef[k + 1]
            row.append((diffuse - drift, diffuse + drift))
        coef.append(row)
    outs = []
    for c in range(3):
        tall = jnp.concatenate([low[c, x], center[c], high[c, x]], axis=0)
        total = center[c] * (3.0 * viscosity * second_coef[0])
        for k in range(1, 5):
            up, down = coef[0][k - 1]
            total = total + v[c, (x + k) & 127] * up + v[c, (x - k) & 127] * down
        for k in range(1, 5):
            up, down = coef[1][k - 1]
            total = total + pltpu.roll(center[c], 128 - k, 1) * up
            total = total + pltpu.roll(center[c], k, 1) * down
        for k in range(1, 5):
            up, down = coef[2][k - 1]
            total = total + tall[reach + k : reach + k + 16] * up
            total = total + tall[reach - k : reach - k + 16] * down
        moved = register[c, x] * section_decay + time_step * total
        register[c, x] = moved
        fluid = center[c] + section_gain * moved
        new_v[c, x] = fluid
        outs.append(fluid)
    return outs


def section_kernel(
    velocity, register, basis, past, owner,
    out_v, out_r, weights, wgram, sheet,
    field, reg, new_v, edge_low, edge_high, low, high, blocks, top, rest, past_v, pieces, ship, rows,
    local, partial, shares, groups, band, full, matrix, sums_ref, fresh, fresh_ship, fresh_in,
    proj_pole, proj_plane, res_pole, res_plane,
    field_sem, reg_sem, halo_send, halo_recv, block_sem, past_sem, piece_send, piece_recv, sum_send, sum_recv,
    out_sem,
):
    group, slab = lax.axis_index("group"), lax.axis_index("slab")
    hello()

    def part_of(chunk):
        return pl.ds(pl.multiple_of(chunk * X_CHUNK, X_CHUNK), X_CHUNK)

    def lanes_of(step):
        return pl.ds(pl.multiple_of(step * CHUNK, CHUNK), CHUNK)

    def field_load(chunk):
        part = part_of(chunk)
        return pltpu.make_async_copy(velocity.at[:, part], field.at[:, part], field_sem.at[chunk])

    def reg_load(chunk):
        part = part_of(chunk)
        return pltpu.make_async_copy(register.at[:, part], reg.at[:, part], reg_sem.at[chunk])

    def block_load(step):
        return pltpu.make_async_copy(basis.at[:, lanes_of(step)], blocks.at[step], block_sem.at[step])

    def start_each(count, make):
        def begin(step, carry):
            make(step).start()
            return carry

        lax.fori_loop(0, count, begin, 0)

    start_each(N_X, field_load)
    past_load = pltpu.make_async_copy(past, past_v, past_sem)
    past_load.start()
    start_each(N_CHUNK, block_load)
    start_each(N_X, reg_load)

    def halo(chunk, side):
        part = part_of(chunk)
        edge, target = ((edge_high, low), (edge_low, high))[side]
        return pltpu.make_async_remote_copy(
            src_ref=edge.at[:, part],
            dst_ref=target.at[:, part],
            send_sem=halo_send.at[side, chunk],
            recv_sem=halo_recv.at[side, chunk],
            device_id=linear((1, -1)[side]),
        )

    def face(chunk, carry):
        field_load(chunk).wait()
        part = part_of(chunk)
        edge_low[:, part] = field[:, part, 0:reach, :]
        edge_high[:, part] = field[:, part, 16 - reach : 16, :]
        return carry

    def face_send(chunk, carry):
        halo(chunk, 0).start()
        halo(chunk, 1).start()
        return carry

    lax.fori_loop(0, N_X, face, 0)
    everyone_in()
    lax.fori_loop(0, N_X, face_send, 0)

    past_load.wait()
    pieces[...] = jnp.zeros_like(pieces)

    def arrange(place, carry):
        piece, plane = place // PLANES, lax.rem(place, PLANES)
        parts = [past_v[:, plane, pl.ds(piece * 4 + j, 1), :].reshape(COUNT - 1, 96) for j in range(4)]
        pieces[piece, plane, 0 : COUNT - 1, :] = jnp.concatenate(parts, axis=1)
        return carry

    lax.fori_loop(0, N_GROUP * PLANES, arrange, 0)

    def pick(step, carry):
        ship[step] = pieces[piece_of(owner, lax.rem(group + step, N_GROUP))]
        return carry

    lax.fori_loop(0, N_GROUP, pick, 0)
    rows[:, group] = ship[0]
    broadcast(
        "group", N_GROUP, lambda step: ship.at[step], rows.at[:, group], piece_send.at[0], piece_recv.at[0]
    )

    local[...] = jnp.zeros_like(local)

    def multiply(step, carry):
        block_load(step).wait()
        upper, lower = split(blocks[step])
        top[step], rest[step] = upper, lower
        local[...] += dot(upper, jnp.concatenate([upper, lower], axis=0), NT)
        return carry

    lax.fori_loop(0, N_CHUNK, multiply, 0)
    cross = local[:, RANK:]
    partial[...] = (local[:, :RANK] + cross + cross.T).reshape(N_SLAB, BAND, RANK)

    def gram_first():
        broadcast(
            "slab", N_SLAB, lambda step: partial.at[lax.rem(slab + step, N_SLAB)], shares.at[slab],
            sum_send.at[0], sum_recv.at[0],
        )
        shares[slab] = partial[slab]

    def gram_second():
        drain(shares.at[pl.ds(0, N_SLAB - 1)], sum_recv.at[0])
        groups[group] = add_slots(shares)
        broadcast(
            "group", N_GROUP, lambda step: groups.at[group], groups.at[group], sum_send.at[1], sum_recv.at[1]
        )

    def gram_third():
        drain(groups.at[pl.ds(0, N_GROUP - 1)], sum_recv.at[1])
        band[...] = add_slots(groups) * (1.0 / (ROWS * N_GROUP * N_SLAB))
        full[slab] = band[...]
        broadcast("slab", N_SLAB, lambda step: band, full.at[slab], sum_send.at[2], sum_recv.at[2])

    def out_copy(chunk, which):
        part = part_of(chunk)
        source, target = ((new_v, out_v), (reg, out_r))[which]
        return pltpu.make_async_copy(source.at[:, part], target.at[:, part], out_sem.at[which, chunk])

    def stencil(chunk, carry):
        halo(chunk, 0).wait_recv()
        halo(chunk, 1).wait_recv()
        reg_load(chunk).wait()

        def coarse(quad, carry):
            x = chunk * X_CHUNK + quad * 4
            sums = column(field, low, high, reg, new_v, x)
            for j in range(1, 4):
                sums = [a + b for a, b in zip(sums, column(field, low, high, reg, new_v, x + j))]
            across = chunk * (X_CHUNK // 4) + quad
            j, piece = lax.rem(across, 4), across // 4
            for c in range(3):
                place = ((c * 4 + j) * N_GROUP + piece) * 16
                sums_ref[pl.ds(pl.multiple_of(place, 16), 16), :] = sums[c]
            return carry

        lax.fori_loop(0, X_CHUNK // 4, coarse, 0)
        out_copy(chunk, 0).start()
        out_copy(chunk, 1).start()
        return carry

    gram_first()
    lax.fori_loop(0, SECOND_AT, stencil, 0)
    gram_second()
    lax.fori_loop(SECOND_AT, THIRD_AT, stencil, 0)
    gram_third()
    lax.fori_loop(THIRD_AT, N_X, stencil, 0)

    fold_fresh(sums_ref, fresh)

    def pick_fresh(step, carry):
        fresh_ship[step] = fresh[piece_of(owner, lax.rem(group + step, N_GROUP))]
        return carry

    lax.fori_loop(0, N_GROUP, pick_fresh, 0)
    fresh_in[group] = fresh_ship[0]
    broadcast(
        "group", N_GROUP, lambda step: fresh_ship.at[step], fresh_in.at[group], piece_send.at[1], piece_recv.at[1]
    )

    drain(full.at[pl.ds(0, N_SLAB - 1)], sum_recv.at[2])
    matrix[...] = full[...].reshape(RANK, RANK)
    invert(matrix, 0, 2)

    drain(ship.at[pl.ds(0, N_GROUP - 1)], piece_recv.at[0])
    drain(fresh_ship.at[pl.ds(0, N_GROUP - 1)], piece_recv.at[1])
    last = lax.broadcasted_iota(jnp.int32, (COUNT, LANES), 0) == COUNT - 1
    for plane in range(PLANES):
        for h in range(N_GROUP):
            start = (plane * N_GROUP + h) * LANES
            sheet[:, start : start + LANES] = jnp.where(
                last, fresh_in[h, plane : plane + 1, :], rows[plane, h]
            )

    def project(step, total):
        head, tail = split(sheet[:, lanes_of(step)])
        both = dot(jnp.concatenate([head, tail], axis=0), top[step], NT)
        return total + both[:COUNT] + both[COUNT:] + dot(head, rest[step], NT)

    proj = lax.fori_loop(0, N_CHUNK, project, jnp.zeros((COUNT, RANK), F32))

    def sum_first(value, pole_ref, place):
        pole = pole_index()
        pole_ref[pole] = value
        broadcast(
            "pole", N_POLE, lambda step: pole_ref.at[pole], pole_ref.at[pole],
            sum_send.at[place], sum_recv.at[place],
        )

    def sum_second(pole_ref, plane_ref, place):
        drain(pole_ref.at[pl.ds(0, N_POLE - 1)], sum_recv.at[place])
        plane = plane_index()
        plane_ref[plane] = add_slots(pole_ref)
        broadcast(
            "plane", N_PLANE, lambda step: plane_ref.at[plane], plane_ref.at[plane],
            sum_send.at[place + 1], sum_recv.at[place + 1],
        )

    def sum_end(plane_ref, place):
        drain(plane_ref.at[pl.ds(0, N_PLANE - 1)], sum_recv.at[place + 1])
        return add_slots(plane_ref) * (1.0 / (ROWS * N_GROUP * N_SLAB))

    sum_first(proj, proj_pole, 3)
    invert(matrix, 2, 4)
    sum_second(proj_pole, proj_plane, 3)
    invert(matrix, 4, RANK // BLOCK)
    proj = sum_end(proj_plane, 3)
    solved = -dot(proj, matrix[...], NN, HIGH)
    weights[...] = solved

    head, tail = split(solved)
    both_parts = jnp.concatenate([head, tail], axis=0)

    def subtract(step, total):
        both = dot(both_parts, top[step], NN)
        image = both[:COUNT] + both[COUNT:] + dot(head, rest[step], NN)
        part = sheet[:, lanes_of(step)] - image
        sheet[:, lanes_of(step)] = part
        return total + dot(part, part, NT, HIGH)

    inner = lax.fori_loop(0, N_CHUNK, subtract, jnp.zeros((COUNT, COUNT), F32))
    sum_first(jnp.concatenate([inner, jnp.zeros((COUNT, 128 - COUNT), F32)], axis=1), res_pole, 5)

    def finish(chunk, carry):
        for which in range(2):
            halo(chunk, which).wait_send()
            out_copy(chunk, which).wait()
        return carry

    lax.fori_loop(0, N_X, finish, 0)
    drain(ship.at[pl.ds(0, N_GROUP - 1)], piece_send.at[0])
    drain(fresh_ship.at[pl.ds(0, N_GROUP - 1)], piece_send.at[1])
    drain(shares.at[pl.ds(0, N_SLAB - 1)], sum_send.at[0])
    drain(groups.at[pl.ds(0, N_GROUP - 1)], sum_send.at[1])
    drain(full.at[pl.ds(0, N_SLAB - 1)], sum_send.at[2])
    drain(proj_pole.at[pl.ds(0, N_POLE - 1)], sum_send.at[3])
    drain(proj_plane.at[pl.ds(0, N_PLANE - 1)], sum_send.at[4])
    sum_second(res_pole, res_plane, 5)
    drain(res_pole.at[pl.ds(0, N_POLE - 1)], sum_send.at[5])
    wgram[...] = sum_end(res_plane, 5)
    drain(res_plane.at[pl.ds(0, N_PLANE - 1)], sum_send.at[6])


SECOND_AT = 4
THIRD_AT = 8


def section(velocity, register, basis, past, owner):
    any_space = pl.BlockSpec(memory_space=pl.ANY)
    vmem = pl.BlockSpec(memory_space=pltpu.VMEM)
    dma = pltpu.SemaphoreType.DMA
    field = (3, 128, 16, 128)
    face = (3, 128, reach, 128)
    pieces = (N_GROUP, PLANES, COUNT, LANES)
    fresh = (N_GROUP, PLANES, LANES)
    scratch = [
        (field, F32), (field, F32), (field, F32), (face, F32), (face, F32), (face, F32), (face, F32),
        ((N_CHUNK, RANK, CHUNK), F32), ((N_CHUNK, RANK, CHUNK), BF16), ((N_CHUNK, RANK, CHUNK), BF16),
        ((COUNT - 1, PLANES, 32, 96), F32), (pieces, F32), (pieces, F32), ((PLANES, N_GROUP, COUNT, LANES), F32),
        ((RANK, 2 * RANK), F32), ((N_SLAB, BAND, RANK), F32), ((N_SLAB, BAND, RANK), F32),
        ((N_GROUP, BAND, RANK), F32), ((BAND, RANK), F32), ((N_SLAB, BAND, RANK), F32), ((RANK, RANK), F32),
        ((1536, 128), F32), (fresh, F32), (fresh, F32), (fresh, F32),
        ((N_POLE, COUNT, RANK), F32), ((N_PLANE, COUNT, RANK), F32),
        ((N_POLE, COUNT, 128), F32), ((N_PLANE, COUNT, 128), F32),
    ]
    semaphores = [(N_X,), (N_X,), (2, N_X), (2, N_X), (N_CHUNK,), None, (2,), (2,), (7,), (7,), (2, N_X)]
    return pl.pallas_call(
        section_kernel,
        in_specs=[any_space] * 4 + [pl.BlockSpec(memory_space=pltpu.SMEM)],
        out_specs=[any_space] * 2 + [vmem] * 3,
        out_shape=[
            jax.ShapeDtypeStruct(field, F32),
            jax.ShapeDtypeStruct(field, F32),
            jax.ShapeDtypeStruct((COUNT, RANK), F32),
            jax.ShapeDtypeStruct((COUNT, 128), F32),
            jax.ShapeDtypeStruct((COUNT, ROWS), F32),
        ],
        scratch_shapes=[pltpu.VMEM(shape, kind) for shape, kind in scratch]
        + [dma if shape is None else dma(shape) for shape in semaphores],
        compiler_params=pltpu.CompilerParams(
            collective_id=0, has_side_effects=True, vmem_limit_bytes=58 * MIB
        ),
        name="section",
    )(velocity, register, basis, past, owner)


def finish_kernel(weights, wgram_ref, residual, coeffs, factor, directions):
    coeffs[...] = weights[...]
    wgram = wgram_ref[...]
    lane = lax.broadcasted_iota(jnp.int32, (COUNT, 128), 1)
    row = lax.broadcasted_iota(jnp.int32, (COUNT, 128), 0)
    lower = jnp.zeros((COUNT, 128), F32)
    inverse = jnp.where(lane == row, 1.0, 0.0)
    for q in range(COUNT):
        scale = lax.rsqrt(wgram[q : q + 1, q : q + 1])
        column = wgram[:, q : q + 1] * scale
        column = jnp.where(row[:, :1] >= q, column, 0.0)
        lower = jnp.where(lane == q, column, lower)
        line = wgram[q : q + 1, :] * scale
        below = jnp.where(row[:, :1] > q, column, 0.0)
        wgram = wgram - below * line
        solved = inverse[q : q + 1, :] * scale
        inverse = jnp.where(row == q, solved, inverse - below * solved)
    factor[...] = lower[:, :COUNT]
    columns = [inverse[:, q : q + 1] for q in range(COUNT)]

    def direct(step, carry):
        lanes = pl.ds(pl.multiple_of(step * CHUNK, CHUNK), CHUNK)
        part = residual[:, lanes]
        total = columns[0] * part[0:1, :]
        for q in range(1, COUNT):
            total = total + columns[q] * part[q : q + 1, :]
        directions[:, lanes] = total
        return carry

    lax.fori_loop(0, N_CHUNK, direct, 0)


def finish(weights, wgram, residual):
    return pl.pallas_call(
        finish_kernel,
        out_shape=[
            jax.ShapeDtypeStruct((COUNT, RANK), F32),
            jax.ShapeDtypeStruct((COUNT, COUNT), F32),
            jax.ShapeDtypeStruct((COUNT, ROWS), F32),
        ],
        name="finish",
    )(weights, wgram, residual)


def local(velocity, register, past, basis, owner):
    new_v, new_r, weights, wgram, residual = section(
        velocity.transpose(0, 1, 3, 2), register.transpose(0, 1, 3, 2), basis.reshape(RANK, ROWS), past, owner.T
    )
    coeffs, factor, directions = finish(weights, wgram, residual)
    return (
        new_v.transpose(0, 1, 3, 2),
        new_r.transpose(0, 1, 3, 2),
        coeffs.T,
        factor,
        directions.reshape(1, 1, COUNT, ROWS),
    )


def solution(mesh):
    in_specs = (
        P(None, None, None, ("group", "slab")),
        P(None, None, None, ("group", "slab")),
        P(None, ("group", "slab"), None, None),
        P("slab", "group", None, None),
        P(),
    )
    out_specs = (
        P(None, None, None, ("group", "slab")),
        P(None, None, None, ("group", "slab")),
        P(),
        P(),
        P("slab", "group", None, None),
    )
    return jax.shard_map(local, mesh=mesh, in_specs=in_specs, out_specs=out_specs, check_vma=False)
```

```python
import functools

import jax
import jax.numpy as jnp
from jax import lax
from jax.experimental import pallas as pl
from jax.experimental.pallas import tpu as pltpu
from jax.sharding import PartitionSpec as P

first_coef = (0.8, -0.2, 4.0 / 105.0, -1.0 / 280.0)
second_coef = (-205.0 / 72.0, 1.6, -0.2, 8.0 / 315.0, -1.0 / 560.0)
time_step = 0.02
viscosity = 0.4
section_decay = -5.0 / 9.0
section_gain = 15.0 / 16.0
reach = 4

F32 = jnp.float32
BF16 = jnp.bfloat16
HIGH = lax.Precision.HIGHEST
NT = (((1,), (1,)), ((), ()))
TN = (((0,), (0,)), ((), ()))
NN = (((1,), (0,)), ((), ()))
N_GROUP = 8
N_SLAB = 16
N_POLE = 8
N_PLANE = 16
N_WALL = 32
N_RING = 4
RANK = 256
ROWS = 12288
COUNT = 8
PLANES = 4
LANES = 384
CHUNK = 1024
N_CHUNK = ROWS // CHUNK
BAND = RANK // N_WALL
X_CHUNK = 16
N_X = 128 // X_CHUNK
BLOCK = 32
MIB = 2**20


def dot(left, right, dims, precision=None):
    return lax.dot_general(
        left, right, dims, precision=precision, preferred_element_type=F32
    )


def split(value):
    high = value.astype(BF16)
    return high, (value - high.astype(F32)).astype(BF16)


def product(left, right, dims):
    def parts(value):
        high, rest = value.astype(BF16), value - value.astype(BF16).astype(F32)
        middle = rest.astype(BF16)
        return high, middle, (rest - middle.astype(F32)).astype(BF16)

    (a, b, c), (d, e, f) = parts(left), parts(right)
    (over_left,), (over_right,) = dims[0]
    return dot(
        jnp.concatenate([a, a, b, b, a, c], axis=over_left),
        jnp.concatenate([d, e, d, e, f, d], axis=over_right),
        dims,
    )


def peer(axis, step):
    group, slab = lax.axis_index("group"), lax.axis_index("slab")
    if axis == "group":
        return (lax.rem(group + step, N_GROUP), slab)
    column = lax.rem(slab // 2, 2)
    if axis == "wall":
        place = lax.rem(wall_index() + step, N_WALL)
        within = lax.rem(place, N_POLE)
        return (group // 4 * 4 + place // N_POLE, within // 2 * 4 + column * 2 + lax.rem(within, 2))
    if axis == "ring":
        place = lax.rem(ring_index() + step, N_RING)
        return (place // 2 * 4 + lax.rem(group, 4), slab - column * 2 + lax.rem(place, 2) * 2)
    if axis == "pole":
        place = lax.rem(pole_index() + step, N_POLE)
        return (group, place // 2 * 4 + column * 2 + lax.rem(place, 2))
    place = lax.rem(plane_index() + step, N_PLANE)
    return (place // 2, slab - column * 2 + lax.rem(place, 2) * 2)


def pole_index():
    slab = lax.axis_index("slab")
    return slab // 4 * 2 + lax.rem(slab, 2)


def wall_index():
    return lax.rem(lax.axis_index("group"), 4) * N_POLE + pole_index()


def ring_index():
    return lax.axis_index("group") // 4 * 2 + lax.rem(lax.axis_index("slab") // 2, 2)


def plane_index():
    return lax.axis_index("group") * 2 + lax.rem(lax.axis_index("slab") // 2, 2)


def linear(step):
    total = N_GROUP * N_SLAB
    place = lax.rem(lax.axis_index("group") * N_SLAB + lax.axis_index("slab") + step + total, total)
    return (place // N_SLAB, lax.rem(place, N_SLAB))


def hello():
    barrier = pltpu.get_barrier_semaphore()
    for axis, size in (("plane", N_PLANE), ("wall", N_WALL)):

        def signal(step, carry, axis=axis):
            pl.semaphore_signal(barrier, inc=1, device_id=peer(axis, step))
            return carry

        lax.fori_loop(1, size, signal, 0)
    for step in (1, -1):
        pl.semaphore_signal(barrier, inc=1, device_id=linear(step))


def everyone_in():
    pl.semaphore_wait(pltpu.get_barrier_semaphore(), N_WALL + N_PLANE)


def broadcast(axis, size, source, target, send_sem, recv_sem):
    def send(step, carry):
        pltpu.make_async_remote_copy(
            src_ref=source(step),
            dst_ref=target,
            send_sem=send_sem,
            recv_sem=recv_sem,
            device_id=peer(axis, step),
        ).start()
        return carry

    lax.fori_loop(1, size, send, 0)


def drain(ref, *sems):
    for sem in sems:
        pltpu.make_async_copy(ref, ref, sem).wait()


def add_slots(ref):
    total = ref[0]
    for slot in range(1, ref.shape[0]):
        total = total + ref[slot]
    return total


def piece_of(owner, group):
    slab = lax.axis_index("slab")
    place = jnp.int32(0)
    for piece in range(N_GROUP):
        place = jnp.where(owner[piece, slab] == group, piece, place)
    return place


def sweep_block(block):
    lane = lax.broadcasted_iota(jnp.int32, (8, 128), 1)
    row = lax.broadcasted_iota(jnp.int32, (8, 128), 0)
    count = block.shape[0] // 8
    parts = [block[8 * i : 8 * i + 8] for i in range(count)]
    for b in range(count):
        line = parts[b]
        columns = [jnp.broadcast_to(line[:, 8 * b + j : 8 * b + j + 1], (8, 128)) for j in range(8)]
        inside = (lane >= 8 * b) & (lane < 8 * b + 8)
        line = jnp.where(inside, jnp.where(lane - 8 * b == row, -1.0, 0.0), line)
        for q in range(8):
            pivot = 1.0 / columns[q][q : q + 1, :]
            solved = line[q : q + 1, :] * pivot
            others = jnp.where(row == q, 0.0, columns[q])
            line = jnp.where(row == q, solved, line - others * solved)
            for j in range(q + 1, 8):
                entry = columns[j][q : q + 1, :] * pivot
                columns[j] = jnp.where(row == q, entry, columns[j] - others * entry)
        for i in range(count):
            if i != b:
                part = parts[i]
                total = jnp.where(inside, 0.0, part)
                for j in range(8):
                    column = jnp.broadcast_to(part[:, 8 * b + j : 8 * b + j + 1], (8, 128))
                    total = total - column * line[j : j + 1, :]
                parts[i] = total
        parts[b] = line
    return -jnp.concatenate(parts, axis=0)


def invert(matrix, first, last):
    lane = lax.broadcasted_iota(jnp.int32, (BLOCK, RANK), 1)
    row = lax.broadcasted_iota(jnp.int32, (BLOCK, RANK), 0)
    wide = lax.broadcasted_iota(jnp.int32, (RANK, RANK), 1)
    for k in range(first, last):
        start = k * BLOCK
        panel = matrix[start : start + BLOCK, :]
        tile = start // 128 * 128
        diagonal = panel[:, tile : tile + 128]
        if start % 128:
            diagonal = pltpu.roll(diagonal, 128 - start % 128, 1)
        inverse = sweep_block(diagonal)[:, :BLOCK]
        inside = (lane >= start) & (lane < start + BLOCK)
        eye = jnp.where(lane - start == row, -1.0, 0.0)
        solved = product(inverse, jnp.where(inside, eye, panel), NN)
        inside = (wide >= start) & (wide < start + BLOCK)
        matrix[...] = jnp.where(inside, 0.0, matrix[...]) - product(panel, solved, TN)
        matrix[start : start + BLOCK, :] = solved


def fold_fresh(sums_ref, fresh):
    rows = sums_ref[pl.ds(0, 384, 4), :]
    for z in range(1, 4):
        rows = rows + sums_ref[pl.ds(z, 384, 4), :]
    row = lax.broadcasted_iota(jnp.int32, (512, 128), 0)
    lane = lax.broadcasted_iota(jnp.int32, (512, 128), 1)
    fold = jnp.where((row // 128 == lane // 32) & ((row % 128) // 4 == lane % 32), 1 / 64, 0.0)
    for tile in range(3):
        parts = []
        for m in range(4):
            j, c = divmod(4 * tile + m, 3)
            parts.append(rows[(c * 4 + j) * 32 : (c * 4 + j) * 32 + 32])
        part = dot(jnp.concatenate(parts, axis=1), fold.astype(F32), NN, HIGH)
        fresh[:, :, tile * 128 : (tile + 1) * 128] = part.reshape(N_GROUP, PLANES, 128)


def column(v, low, high, register, new_v, x):
    center = [v[c, x] for c in range(3)]
    coef = []
    for axis in range(3):
        row = []
        for k in range(4):
            drift = center[axis] * first_coef[k]
            diffuse = viscosity * second_coef[k + 1]
            row.append((diffuse - drift, diffuse + drift))
        coef.append(row)
    outs = []
    for c in range(3):
        tall = jnp.concatenate([low[c, x], center[c], high[c, x]], axis=0)
        total = center[c] * (3.0 * viscosity * second_coef[0])
        for k in range(1, 5):
            up, down = coef[0][k - 1]
            total = total + v[c, (x + k) & 127] * up + v[c, (x - k) & 127] * down
        for k in range(1, 5):
            up, down = coef[1][k - 1]
            total = total + pltpu.roll(center[c], 128 - k, 1) * up
            total = total + pltpu.roll(center[c], k, 1) * down
        for k in range(1, 5):
            up, down = coef[2][k - 1]
            total = total + tall[reach + k : reach + k + 16] * up
            total = total + tall[reach - k : reach - k + 16] * down
        moved = register[c, x] * section_decay + time_step * total
        register[c, x] = moved
        fluid = center[c] + section_gain * moved
        new_v[c, x] = fluid
        outs.append(fluid)
    return outs


def section_kernel(
    velocity, register, basis, past, owner,
    new_v, reg, weights, wgram, sheet,
    field, edge_low, edge_high, low, high, blocks, top, rest, past_v, pieces, ship, rows,
    local, partial, shares, rings, band, full, matrix, sums_ref, fresh, fresh_ship, fresh_in,
    proj_pole, proj_plane, res_pole, res_plane,
    field_sem, reg_sem, halo_send, halo_recv, block_sem, past_sem, piece_send, piece_recv, sum_send, sum_recv,
):
    group = lax.axis_index("group")

    def part_of(chunk):
        return pl.ds(pl.multiple_of(chunk * X_CHUNK, X_CHUNK), X_CHUNK)

    def lanes_of(step):
        return pl.ds(pl.multiple_of(step * CHUNK, CHUNK), CHUNK)

    def field_load(chunk):
        part = part_of(chunk)
        return pltpu.make_async_copy(velocity.at[:, part], field.at[:, part], field_sem.at[chunk])

    def reg_load(chunk):
        part = part_of(chunk)
        return pltpu.make_async_copy(register.at[:, part], reg.at[:, part], reg_sem.at[chunk])

    def block_load(step):
        return pltpu.make_async_copy(basis.at[:, lanes_of(step)], blocks.at[step], block_sem.at[step])

    def start_each(count, make):
        def begin(step, carry):
            make(step).start()
            return carry

        lax.fori_loop(0, count, begin, 0)

    start_each(N_X, field_load)
    hello()
    past_load = pltpu.make_async_copy(past, past_v, past_sem)
    start_each(N_CHUNK, block_load)
    past_load.start()
    start_each(N_X, reg_load)

    def halo(chunk, side):
        part = part_of(chunk)
        edge, target = ((edge_high, low), (edge_low, high))[side]
        return pltpu.make_async_remote_copy(
            src_ref=edge.at[:, part],
            dst_ref=target.at[:, part],
            send_sem=halo_send.at[side, chunk],
            recv_sem=halo_recv.at[side, chunk],
            device_id=linear((1, -1)[side]),
        )

    def face(chunk, carry):
        field_load(chunk).wait()
        part = part_of(chunk)
        edge_low[:, part] = field[:, part, 0:reach, :]
        edge_high[:, part] = field[:, part, 16 - reach : 16, :]
        return carry

    def face_send(chunk, carry):
        halo(chunk, 0).start()
        halo(chunk, 1).start()
        return carry

    lax.fori_loop(0, N_X, face, 0)

    local[...] = jnp.zeros_like(local)

    def multiply(step, carry):
        block_load(step).wait()
        upper, lower = split(blocks[step])
        top[step], rest[step] = upper, lower
        local[...] += dot(upper, jnp.concatenate([upper, lower], axis=0), NT)
        return carry

    lax.fori_loop(0, GRAM_FIRST, multiply, 0)
    everyone_in()
    lax.fori_loop(0, AHEAD, face_send, 0)
    lax.fori_loop(GRAM_FIRST, N_CHUNK, multiply, 0)
    cross = local[:, RANK:]
    partial[...] = (local[:, :RANK] + cross + cross.T).reshape(N_WALL, BAND, RANK)

    wall, ring = wall_index(), ring_index()

    def gram_first():
        broadcast(
            "wall", N_WALL, lambda step: partial.at[lax.rem(wall + step, N_WALL)], shares.at[wall],
            sum_send.at[0], sum_recv.at[0],
        )
        shares[wall] = partial[wall]

    def gram_second():
        drain(shares.at[pl.ds(0, N_WALL - 1)], sum_recv.at[0])
        rings[ring] = add_slots(shares)
        broadcast(
            "ring", N_RING, lambda step: rings.at[ring], rings.at[ring], sum_send.at[1], sum_recv.at[1]
        )

    def gram_third():
        drain(rings.at[pl.ds(0, N_RING - 1)], sum_recv.at[1])
        band[...] = add_slots(rings) * (1.0 / (ROWS * N_GROUP * N_SLAB))
        full[wall] = band[...]
        broadcast("wall", N_WALL, lambda step: band, full.at[wall], sum_send.at[2], sum_recv.at[2])

    gram_first()

    past_load.wait()
    pieces[...] = jnp.zeros_like(pieces)

    def arrange(place, carry):
        piece, plane = place // PLANES, lax.rem(place, PLANES)
        parts = [past_v[:, plane, pl.ds(piece * 4 + j, 1), :].reshape(COUNT - 1, 96) for j in range(4)]
        pieces[piece, plane, 0 : COUNT - 1, :] = jnp.concatenate(parts, axis=1)
        return carry

    lax.fori_loop(0, N_GROUP * PLANES, arrange, 0)

    def pick(step, carry):
        ship[step] = pieces[piece_of(owner, lax.rem(group + step, N_GROUP))]
        return carry

    lax.fori_loop(0, N_GROUP, pick, 0)
    rows[:, group] = ship[0]
    broadcast(
        "group", N_GROUP, lambda step: ship.at[step], rows.at[:, group], piece_send.at[0], piece_recv.at[0]
    )

    def stencil(chunk, carry):
        halo(chunk, 0).wait_recv()
        halo(chunk, 1).wait_recv()
        reg_load(chunk).wait()

        @pl.when(chunk + AHEAD < N_X)
        def _():
            face_send(chunk + AHEAD, 0)

        def coarse(quad, carry):
            x = chunk * X_CHUNK + quad * 4
            sums = column(field, low, high, reg, new_v, x)
            for j in range(1, 4):
                sums = [a + b for a, b in zip(sums, column(field, low, high, reg, new_v, x + j))]
            across = chunk * (X_CHUNK // 4) + quad
            j, piece = lax.rem(across, 4), across // 4
            for c in range(3):
                place = ((c * 4 + j) * N_GROUP + piece) * 16
                sums_ref[pl.ds(pl.multiple_of(place, 16), 16), :] = sums[c]
            return carry

        lax.fori_loop(0, X_CHUNK // 4, coarse, 0)
        return carry

    lax.fori_loop(0, SECOND_AT, stencil, 0)
    gram_second()
    lax.fori_loop(SECOND_AT, THIRD_AT, stencil, 0)
    gram_third()
    lax.fori_loop(THIRD_AT, N_X, stencil, 0)

    fold_fresh(sums_ref, fresh)

    def pick_fresh(step, carry):
        fresh_ship[step] = fresh[piece_of(owner, lax.rem(group + step, N_GROUP))]
        return carry

    lax.fori_loop(0, N_GROUP, pick_fresh, 0)
    fresh_in[group] = fresh_ship[0]
    broadcast(
        "group", N_GROUP, lambda step: fresh_ship.at[step], fresh_in.at[group], piece_send.at[1], piece_recv.at[1]
    )

    drain(ship.at[pl.ds(0, N_GROUP - 1)], piece_recv.at[0])
    places = [(plane, h) for plane in range(PLANES) for h in range(N_GROUP)]
    for at, (plane, h) in enumerate(places):
        sheet[:, at * LANES : (at + 1) * LANES] = rows[plane, h]

    def project(step, total):
        head, tail = split(sheet[:, lanes_of(step)])
        both = dot(top[step], jnp.concatenate([head, tail], axis=0), NT)
        return total + both[:, :COUNT] + both[:, COUNT:] + dot(rest[step], head, NT)

    past_proj = lax.fori_loop(0, N_CHUNK, project, jnp.zeros((RANK, COUNT), F32), unroll=4)

    drain(full.at[pl.ds(0, N_WALL - 1)], sum_recv.at[2])
    matrix[...] = full[...].reshape(RANK, RANK)
    invert(matrix, 0, 1)

    drain(fresh_ship.at[pl.ds(0, N_GROUP - 1)], piece_recv.at[1])
    for at, (plane, h) in enumerate(places):
        sheet[COUNT - 1 : COUNT, at * LANES : (at + 1) * LANES] = fresh_in[h, plane : plane + 1, :]

    def project_fresh(step, total):
        line = sheet[COUNT - 1 : COUNT, lanes_of(step)]
        block = blocks[step]
        for q in range(CHUNK // 128):
            total = total + block[:, q * 128 : (q + 1) * 128] * line[:, q * 128 : (q + 1) * 128]
        return total

    fresh_proj = lax.fori_loop(0, N_CHUNK, project_fresh, jnp.zeros((RANK, 128), F32))
    fresh_proj = jnp.sum(fresh_proj, axis=1, keepdims=True)
    which = lax.broadcasted_iota(jnp.int32, (RANK, COUNT), 1)
    proj = jnp.where(which == COUNT - 1, fresh_proj, past_proj).T

    def sum_first(value, pole_ref, place):
        pole = pole_index()
        pole_ref[pole] = value
        broadcast(
            "pole", N_POLE, lambda step: pole_ref.at[pole], pole_ref.at[pole],
            sum_send.at[place], sum_recv.at[place],
        )

    def sum_second(pole_ref, plane_ref, place):
        drain(pole_ref.at[pl.ds(0, N_POLE - 1)], sum_recv.at[place])
        plane = plane_index()
        plane_ref[plane] = add_slots(pole_ref)
        broadcast(
            "plane", N_PLANE, lambda step: plane_ref.at[plane], plane_ref.at[plane],
            sum_send.at[place + 1], sum_recv.at[place + 1],
        )

    def sum_end(plane_ref, place):
        drain(plane_ref.at[pl.ds(0, N_PLANE - 1)], sum_recv.at[place + 1])
        return add_slots(plane_ref) * (1.0 / (ROWS * N_GROUP * N_SLAB))

    sum_first(proj, proj_pole, 3)
    invert(matrix, 1, 3)
    sum_second(proj_pole, proj_plane, 3)
    invert(matrix, 3, RANK // BLOCK)
    proj = sum_end(proj_plane, 3)
    solved = -dot(proj, matrix[...], NN, HIGH)
    weights[...] = solved

    head, tail = split(solved)
    both_parts = jnp.concatenate([head, tail], axis=0)

    def subtract(step, total):
        both = dot(both_parts, top[step], NN)
        image = both[:COUNT] + both[COUNT:] + dot(head, rest[step], NN)
        part = sheet[:, lanes_of(step)] - image
        sheet[:, lanes_of(step)] = part
        return total + dot(part, part, NT, HIGH)

    inner = lax.fori_loop(0, N_CHUNK, subtract, jnp.zeros((COUNT, COUNT), F32), unroll=4)
    sum_first(jnp.concatenate([inner, jnp.zeros((COUNT, 128 - COUNT), F32)], axis=1), res_pole, 5)

    def finish(chunk, carry):
        for which in range(2):
            halo(chunk, which).wait_send()
        return carry

    lax.fori_loop(0, N_X, finish, 0)
    drain(ship.at[pl.ds(0, N_GROUP - 1)], piece_send.at[0])
    drain(fresh_ship.at[pl.ds(0, N_GROUP - 1)], piece_send.at[1])
    drain(shares.at[pl.ds(0, N_WALL - 1)], sum_send.at[0])
    drain(rings.at[pl.ds(0, N_RING - 1)], sum_send.at[1])
    drain(full.at[pl.ds(0, N_WALL - 1)], sum_send.at[2])
    drain(proj_pole.at[pl.ds(0, N_POLE - 1)], sum_send.at[3])
    drain(proj_plane.at[pl.ds(0, N_PLANE - 1)], sum_send.at[4])
    sum_second(res_pole, res_plane, 5)
    drain(res_pole.at[pl.ds(0, N_POLE - 1)], sum_send.at[5])
    wgram[...] = sum_end(res_plane, 5)
    drain(res_plane.at[pl.ds(0, N_PLANE - 1)], sum_send.at[6])


AHEAD = 4
GRAM_FIRST = 6
SECOND_AT, THIRD_AT = 3, 6


def section(velocity, register, basis, past, owner):
    hbm = pl.BlockSpec(memory_space=pltpu.HBM)
    vmem = pl.BlockSpec(memory_space=pltpu.VMEM)
    dma = pltpu.SemaphoreType.DMA
    field = (3, 128, 16, 128)
    face = (3, 128, reach, 128)
    pieces = (N_GROUP, PLANES, COUNT, LANES)
    fresh = (N_GROUP, PLANES, LANES)
    scratch = [
        (field, F32), (face, F32), (face, F32), (face, F32), (face, F32),
        ((N_CHUNK, RANK, CHUNK), F32), ((N_CHUNK, RANK, CHUNK), BF16), ((N_CHUNK, RANK, CHUNK), BF16),
        ((COUNT - 1, PLANES, 32, 96), F32), (pieces, F32), (pieces, F32), ((PLANES, N_GROUP, COUNT, LANES), F32),
        ((RANK, 2 * RANK), F32), ((N_WALL, BAND, RANK), F32), ((N_WALL, BAND, RANK), F32),
        ((N_RING, BAND, RANK), F32), ((BAND, RANK), F32), ((N_WALL, BAND, RANK), F32), ((RANK, RANK), F32),
        ((1536, 128), F32), (fresh, F32), (fresh, F32), (fresh, F32),
        ((N_POLE, COUNT, RANK), F32), ((N_PLANE, COUNT, RANK), F32),
        ((N_POLE, COUNT, 128), F32), ((N_PLANE, COUNT, 128), F32),
    ]
    semaphores = [(N_X,), (N_X,), (2, N_X), (2, N_X), (N_CHUNK,), None, (2,), (2,), (7,), (7,)]
    return pl.pallas_call(
        section_kernel,
        in_specs=[hbm] * 4 + [pl.BlockSpec(memory_space=pltpu.SMEM)],
        out_specs=[vmem] * 5,
        out_shape=[
            pltpu.VMEM(shape, F32)
            for shape in (field, field, (COUNT, RANK), (COUNT, 128), (COUNT, ROWS))
        ],
        scratch_shapes=[pltpu.VMEM(shape, kind) for shape, kind in scratch]
        + [dma if shape is None else dma(shape) for shape in semaphores],
        compiler_params=pltpu.CompilerParams(
            collective_id=0, has_side_effects=True, vmem_limit_bytes=46 * MIB
        ),
        name="section",
    )(velocity, register, basis, past, owner)


def finish_kernel(new_v, reg, weights, wgram_ref, residual, out_v, out_r, coeffs, factor, directions, sems):
    copies = [
        pltpu.make_async_copy(source, target, sems.at[i])
        for i, (source, target) in enumerate(((new_v, out_v), (reg, out_r)))
    ]
    for copy in copies:
        copy.start()
    coeffs[...] = weights[...]
    wgram = wgram_ref[...]
    lane = lax.broadcasted_iota(jnp.int32, (COUNT, 128), 1)
    row = lax.broadcasted_iota(jnp.int32, (COUNT, 128), 0)
    lower = jnp.zeros((COUNT, 128), F32)
    inverse = jnp.where(lane == row, 1.0, 0.0)
    for q in range(COUNT):
        scale = lax.rsqrt(wgram[q : q + 1, q : q + 1])
        column = wgram[:, q : q + 1] * scale
        column = jnp.where(row[:, :1] >= q, column, 0.0)
        lower = jnp.where(lane == q, column, lower)
        line = wgram[q : q + 1, :] * scale
        below = jnp.where(row[:, :1] > q, column, 0.0)
        wgram = wgram - below * line
        solved = inverse[q : q + 1, :] * scale
        inverse = jnp.where(row == q, solved, inverse - below * solved)
    factor[...] = lower[:, :COUNT]
    columns = [inverse[:, q : q + 1] for q in range(COUNT)]

    def direct(step, carry):
        lanes = pl.ds(pl.multiple_of(step * CHUNK, CHUNK), CHUNK)
        part = residual[:, lanes]
        total = columns[0] * part[0:1, :]
        for q in range(1, COUNT):
            total = total + columns[q] * part[q : q + 1, :]
        directions[:, lanes] = total
        return carry

    lax.fori_loop(0, N_CHUNK, direct, 0)
    for copy in copies:
        copy.wait()


def finish(*operands):
    operands = [pltpu.with_memory_space_constraint(operand, pltpu.VMEM) for operand in operands]
    vmem = pl.BlockSpec(memory_space=pltpu.VMEM)
    return pl.pallas_call(
        finish_kernel,
        out_shape=[
            jax.ShapeDtypeStruct((3, 128, 16, 128), F32),
            jax.ShapeDtypeStruct((3, 128, 16, 128), F32),
            jax.ShapeDtypeStruct((COUNT, RANK), F32),
            jax.ShapeDtypeStruct((COUNT, COUNT), F32),
            jax.ShapeDtypeStruct((COUNT, ROWS), F32),
        ],
        in_specs=[vmem] * 5,
        out_specs=[pl.BlockSpec(memory_space=pl.ANY)] * 2 + [vmem] * 3,
        scratch_shapes=[pltpu.SemaphoreType.DMA((2,))],
        compiler_params=pltpu.CompilerParams(vmem_limit_bytes=8 * MIB),
        name="finish",
    )(*operands)


def local(velocity, register, past, basis, owner):
    operands = section(
        velocity.transpose(0, 1, 3, 2),
        register.transpose(0, 1, 3, 2),
        basis.reshape(RANK, ROWS),
        pltpu.with_memory_space_constraint(past, pltpu.HBM),
        pltpu.with_memory_space_constraint(owner.T, pltpu.HBM),
    )
    new_v, new_r, coeffs, factor, directions = finish(*operands)
    return (
        new_v.transpose(0, 1, 3, 2),
        new_r.transpose(0, 1, 3, 2),
        coeffs.T,
        factor,
        directions.reshape(1, 1, COUNT, ROWS),
    )


def solution(mesh):
    in_specs = (
        P(None, None, None, ("group", "slab")),
        P(None, None, None, ("group", "slab")),
        P(None, ("group", "slab"), None, None),
        P("slab", "group", None, None),
        P(),
    )
    out_specs = (
        P(None, None, None, ("group", "slab")),
        P(None, None, None, ("group", "slab")),
        P(),
        P(),
        P("slab", "group", None, None),
    )
    return jax.shard_map(local, mesh=mesh, in_specs=in_specs, out_specs=out_specs, check_vma=False)
```

```python
import functools

import jax
import jax.numpy as jnp
from jax import lax
from jax.experimental import pallas as pl
from jax.experimental.pallas import tpu as pltpu
from jax.sharding import PartitionSpec as P

first_coef = (0.8, -0.2, 4.0 / 105.0, -1.0 / 280.0)
second_coef = (-205.0 / 72.0, 1.6, -0.2, 8.0 / 315.0, -1.0 / 560.0)
time_step = 0.02
viscosity = 0.4
section_decay = -5.0 / 9.0
section_gain = 15.0 / 16.0
reach = 4

F32 = jnp.float32
BF16 = jnp.bfloat16
HIGH = lax.Precision.HIGHEST
NT = (((1,), (1,)), ((), ()))
TN = (((0,), (0,)), ((), ()))
NN = (((1,), (0,)), ((), ()))
N_GROUP = 8
N_SLAB = 16
N_POLE = 8
N_PLANE = 16
N_WALL = 32
N_RING = 4
RANK = 256
ROWS = 12288
COUNT = 8
PLANES = 4
LANES = 384
CHUNK = 1024
N_CHUNK = ROWS // CHUNK
BAND = RANK // N_WALL
X_CHUNK = 16
N_X = 128 // X_CHUNK
BLOCK = 32
MIB = 2**20


def dot(left, right, dims, precision=None):
    return lax.dot_general(
        left, right, dims, precision=precision, preferred_element_type=F32
    )


def split(value):
    high = value.astype(BF16)
    return high, (value - high.astype(F32)).astype(BF16)


def in_parts(value):
    high, rest = value.astype(BF16), value - value.astype(BF16).astype(F32)
    middle = rest.astype(BF16)
    return high, middle, (rest - middle.astype(F32)).astype(BF16)


def product(left, right, dims):
    (a, b, c), (d, e, f) = in_parts(left), in_parts(right)
    (over_left,), (over_right,) = dims[0]
    return dot(
        jnp.concatenate([a, a, b, b, a, c], axis=over_left),
        jnp.concatenate([d, e, d, e, f, d], axis=over_right),
        dims,
    )


def peer(axis, step):
    group, slab = lax.axis_index("group"), lax.axis_index("slab")
    if axis == "group":
        return (lax.rem(group + step, N_GROUP), slab)
    column = lax.rem(slab // 2, 2)
    if axis == "wall":
        place = lax.rem(wall_index() + step, N_WALL)
        within = lax.rem(place, N_POLE)
        return (group // 4 * 4 + place // N_POLE, within // 2 * 4 + column * 2 + lax.rem(within, 2))
    if axis == "ring":
        place = lax.rem(ring_index() + step, N_RING)
        return (place // 2 * 4 + lax.rem(group, 4), slab - column * 2 + lax.rem(place, 2) * 2)
    if axis == "pole":
        place = lax.rem(pole_index() + step, N_POLE)
        return (group, place // 2 * 4 + column * 2 + lax.rem(place, 2))
    place = lax.rem(plane_index() + step, N_PLANE)
    return (place // 2, slab - column * 2 + lax.rem(place, 2) * 2)


def pole_index():
    slab = lax.axis_index("slab")
    return slab // 4 * 2 + lax.rem(slab, 2)


def wall_index():
    return lax.rem(lax.axis_index("group"), 4) * N_POLE + pole_index()


def ring_index():
    return lax.axis_index("group") // 4 * 2 + lax.rem(lax.axis_index("slab") // 2, 2)


def plane_index():
    return lax.axis_index("group") * 2 + lax.rem(lax.axis_index("slab") // 2, 2)


def linear(step):
    total = N_GROUP * N_SLAB
    place = lax.rem(lax.axis_index("group") * N_SLAB + lax.axis_index("slab") + step + total, total)
    return (place // N_SLAB, lax.rem(place, N_SLAB))


def hello():
    barrier = pltpu.get_barrier_semaphore()
    for axis, size in (("plane", N_PLANE), ("wall", N_WALL)):

        def signal(step, carry, axis=axis):
            pl.semaphore_signal(barrier, inc=1, device_id=peer(axis, step))
            return carry

        lax.fori_loop(1, size, signal, 0)
    for step in (1, -1):
        pl.semaphore_signal(barrier, inc=1, device_id=linear(step))


def everyone_in():
    pl.semaphore_wait(pltpu.get_barrier_semaphore(), N_WALL + N_PLANE)


def broadcast(axis, size, source, target, send_sem, recv_sem):
    def send(step, carry):
        pltpu.make_async_remote_copy(
            src_ref=source(step),
            dst_ref=target,
            send_sem=send_sem,
            recv_sem=recv_sem,
            device_id=peer(axis, step),
        ).start()
        return carry

    lax.fori_loop(1, size, send, 0)


def drain(ref, *sems):
    for sem in sems:
        pltpu.make_async_copy(ref, ref, sem).wait()


def add_slots(ref):
    total = ref[0]
    for slot in range(1, ref.shape[0]):
        total = total + ref[slot]
    return total


def piece_of(owner, group):
    slab = lax.axis_index("slab")
    place = jnp.int32(0)
    for piece in range(N_GROUP):
        place = jnp.where(owner[piece, slab] == group, piece, place)
    return place


def sweep_block(block):
    lane = lax.broadcasted_iota(jnp.int32, (8, 128), 1)
    row = lax.broadcasted_iota(jnp.int32, (8, 128), 0)
    count = block.shape[0] // 8
    parts = [block[8 * i : 8 * i + 8] for i in range(count)]
    for b in range(count):
        line = parts[b]
        columns = [jnp.broadcast_to(line[:, 8 * b + j : 8 * b + j + 1], (8, 128)) for j in range(8)]
        inside = (lane >= 8 * b) & (lane < 8 * b + 8)
        line = jnp.where(inside, jnp.where(lane - 8 * b == row, -1.0, 0.0), line)
        for q in range(8):
            pivot = 1.0 / columns[q][q : q + 1, :]
            solved = line[q : q + 1, :] * pivot
            others = jnp.where(row == q, 0.0, columns[q])
            line = jnp.where(row == q, solved, line - others * solved)
            for j in range(q + 1, 8):
                entry = columns[j][q : q + 1, :] * pivot
                columns[j] = jnp.where(row == q, entry, columns[j] - others * entry)
        for i in range(count):
            if i != b:
                part = parts[i]
                total = jnp.where(inside, 0.0, part)
                for j in range(8):
                    column = jnp.broadcast_to(part[:, 8 * b + j : 8 * b + j + 1], (8, 128))
                    total = total - column * line[j : j + 1, :]
                parts[i] = total
        parts[b] = line
    return -jnp.concatenate(parts, axis=0)


def invert(matrix, first, last):
    lane = lax.broadcasted_iota(jnp.int32, (BLOCK, RANK), 1)
    row = lax.broadcasted_iota(jnp.int32, (BLOCK, RANK), 0)
    wide = lax.broadcasted_iota(jnp.int32, (RANK, RANK), 1)
    for k in range(first, last):
        start = k * BLOCK
        panel = matrix[start : start + BLOCK, :]
        tile = start // 128 * 128
        diagonal = panel[:, tile : tile + 128]
        if start % 128:
            diagonal = pltpu.roll(diagonal, 128 - start % 128, 1)
        inverse = sweep_block(diagonal)[:, :BLOCK]
        inside = (lane >= start) & (lane < start + BLOCK)
        eye = jnp.where(lane - start == row, -1.0, 0.0)
        solved = product(inverse, jnp.where(inside, eye, panel), NN)
        inside = (wide >= start) & (wide < start + BLOCK)
        matrix[...] = jnp.where(inside, 0.0, matrix[...]) - product(panel, solved, TN)
        matrix[start : start + BLOCK, :] = solved


def fold_fresh(sums_ref, fresh):
    rows = sums_ref[pl.ds(0, 384, 4), :]
    for z in range(1, 4):
        rows = rows + sums_ref[pl.ds(z, 384, 4), :]
    row = lax.broadcasted_iota(jnp.int32, (512, 128), 0)
    lane = lax.broadcasted_iota(jnp.int32, (512, 128), 1)
    fold = jnp.where((row // 128 == lane // 32) & ((row % 128) // 4 == lane % 32), 1 / 64, 0.0).astype(BF16)
    tiles = []
    for tile in range(3):
        parts = []
        for m in range(4):
            j, c = divmod(4 * tile + m, 3)
            parts.append(rows[(c * 4 + j) * 32 : (c * 4 + j) * 32 + 32])
        tiles.append(jnp.concatenate(parts, axis=1))
    boxes = jnp.concatenate(tiles, axis=0)
    means = dot(jnp.concatenate(in_parts(boxes), axis=0), fold, NN)
    means = means[:96] + (means[96:192] + means[192:])
    for tile in range(3):
        part = means[tile * 32 : (tile + 1) * 32]
        fresh[:, :, tile * 128 : (tile + 1) * 128] = part.reshape(N_GROUP, PLANES, 128)


def column(v, low, high, register, new_v, x):
    center = [v[c, x] for c in range(3)]
    coef = []
    for axis in range(3):
        row = []
        for k in range(4):
            drift = center[axis] * first_coef[k]
            diffuse = viscosity * second_coef[k + 1]
            row.append((diffuse - drift, diffuse + drift))
        coef.append(row)
    outs = []
    for c in range(3):
        tall = jnp.concatenate([low[c, x], center[c], high[c, x]], axis=0)
        total = center[c] * (3.0 * viscosity * second_coef[0])
        for k in range(1, 5):
            up, down = coef[0][k - 1]
            total = total + v[c, (x + k) & 127] * up + v[c, (x - k) & 127] * down
        for k in range(1, 5):
            up, down = coef[1][k - 1]
            total = total + pltpu.roll(center[c], 128 - k, 1) * up
            total = total + pltpu.roll(center[c], k, 1) * down
        for k in range(1, 5):
            up, down = coef[2][k - 1]
            total = total + tall[reach + k : reach + k + 16] * up
            total = total + tall[reach - k : reach - k + 16] * down
        moved = register[c, x] * section_decay + time_step * total
        register[c, x] = moved
        fluid = center[c] + section_gain * moved
        new_v[c, x] = fluid
        outs.append(fluid)
    return outs


def section_kernel(
    velocity, register, basis, past, owner,
    new_v, reg, weights, wgram, sheet,
    field, edge_low, edge_high, low, high, blocks, top, rest, past_v, pieces, ship, rows,
    local, partial, shares, rings, band, full, matrix, sums_ref, fresh, fresh_ship, fresh_in,
    proj_pole, proj_plane, res_pole, res_plane,
    field_sem, reg_sem, halo_send, halo_recv, block_sem, past_sem, piece_send, piece_recv, sum_send, sum_recv,
):
    group = lax.axis_index("group")

    def part_of(chunk):
        return pl.ds(pl.multiple_of(chunk * X_CHUNK, X_CHUNK), X_CHUNK)

    def lanes_of(step):
        return pl.ds(pl.multiple_of(step * CHUNK, CHUNK), CHUNK)

    def field_load(chunk):
        part = part_of(chunk)
        return pltpu.make_async_copy(velocity.at[:, part], field.at[:, part], field_sem.at[chunk])

    def reg_load(chunk):
        part = part_of(chunk)
        return pltpu.make_async_copy(register.at[:, part], reg.at[:, part], reg_sem.at[chunk])

    def block_load(step):
        return pltpu.make_async_copy(basis.at[:, lanes_of(step)], blocks.at[step], block_sem.at[step])

    def start_each(count, make):
        def begin(step, carry):
            make(step).start()
            return carry

        lax.fori_loop(0, count, begin, 0)

    start_each(N_X, field_load)
    hello()
    past_load = pltpu.make_async_copy(past, past_v, past_sem)
    start_each(N_CHUNK, block_load)
    past_load.start()
    start_each(N_X, reg_load)

    def halo(chunk, side):
        part = part_of(chunk)
        edge, target = ((edge_high, low), (edge_low, high))[side]
        return pltpu.make_async_remote_copy(
            src_ref=edge.at[:, part],
            dst_ref=target.at[:, part],
            send_sem=halo_send.at[side, chunk],
            recv_sem=halo_recv.at[side, chunk],
            device_id=linear((1, -1)[side]),
        )

    def face(chunk, carry):
        field_load(chunk).wait()
        part = part_of(chunk)
        edge_low[:, part] = field[:, part, 0:reach, :]
        edge_high[:, part] = field[:, part, 16 - reach : 16, :]
        return carry

    def face_send(chunk, carry):
        halo(chunk, 0).start()
        halo(chunk, 1).start()
        return carry

    lax.fori_loop(0, N_X, face, 0)

    local[...] = jnp.zeros_like(local)

    def multiply(step, carry):
        block_load(step).wait()
        upper, lower = split(blocks[step])
        top[step], rest[step] = upper, lower
        local[...] += dot(upper, jnp.concatenate([upper, lower], axis=0), NT)
        return carry

    lax.fori_loop(0, GRAM_FIRST, multiply, 0)
    everyone_in()
    lax.fori_loop(0, FIRST, face_send, 0)
    lax.fori_loop(GRAM_FIRST, N_CHUNK, multiply, 0)
    cross = local[:, RANK:]
    partial[...] = (local[:, :RANK] + cross + cross.T).reshape(N_WALL, BAND, RANK)

    wall, ring = wall_index(), ring_index()

    def gram_first():
        broadcast(
            "wall", N_WALL, lambda step: partial.at[lax.rem(wall + step, N_WALL)], shares.at[wall],
            sum_send.at[0], sum_recv.at[0],
        )
        shares[wall] = partial[wall]

    def gram_second():
        drain(shares.at[pl.ds(0, N_WALL - 1)], sum_recv.at[0])
        rings[ring] = add_slots(shares)
        broadcast(
            "ring", N_RING, lambda step: rings.at[ring], rings.at[ring], sum_send.at[1], sum_recv.at[1]
        )

    def gram_third():
        drain(rings.at[pl.ds(0, N_RING - 1)], sum_recv.at[1])
        band[...] = add_slots(rings) * (1.0 / (ROWS * N_GROUP * N_SLAB))
        full[wall] = band[...]
        broadcast("wall", N_WALL, lambda step: band, full.at[wall], sum_send.at[2], sum_recv.at[2])

    gram_first()
    lax.fori_loop(FIRST, AHEAD, face_send, 0)

    past_load.wait()
    pieces[...] = jnp.zeros_like(pieces)

    def arrange(place, carry):
        piece, plane = place // PLANES, lax.rem(place, PLANES)
        parts = [past_v[:, plane, pl.ds(piece * 4 + j, 1), :].reshape(COUNT - 1, 96) for j in range(4)]
        pieces[piece, plane, 0 : COUNT - 1, :] = jnp.concatenate(parts, axis=1)
        return carry

    lax.fori_loop(0, N_GROUP * PLANES, arrange, 0)

    def pick(step, carry):
        ship[step] = pieces[piece_of(owner, lax.rem(group + step, N_GROUP))]
        return carry

    lax.fori_loop(0, N_GROUP, pick, 0)
    rows[:, group] = ship[0]

    def ship_past():
        broadcast(
            "group", N_GROUP, lambda step: ship.at[step], rows.at[:, group], piece_send.at[0], piece_recv.at[0]
        )

    def arrive(chunk):
        halo(chunk, 0).wait_recv()
        halo(chunk, 1).wait_recv()
        reg_load(chunk).wait()

    def stencil(chunk, carry):
        arrive(chunk)
        return advance(chunk, carry)

    def advance(chunk, carry):

        @pl.when(chunk + AHEAD < N_X)
        def _():
            face_send(chunk + AHEAD, 0)

        def coarse(quad, carry):
            x = chunk * X_CHUNK + quad * 4
            sums = column(field, low, high, reg, new_v, x)
            for j in range(1, 4):
                sums = [a + b for a, b in zip(sums, column(field, low, high, reg, new_v, x + j))]
            across = chunk * (X_CHUNK // 4) + quad
            j, piece = lax.rem(across, 4), across // 4
            for c in range(3):
                place = ((c * 4 + j) * N_GROUP + piece) * 16
                sums_ref[pl.ds(pl.multiple_of(place, 16), 16), :] = sums[c]
            return carry

        lax.fori_loop(0, X_CHUNK // 4, coarse, 0)
        return carry

    lax.fori_loop(0, SECOND_AT, stencil, 0)
    gram_second()
    lax.fori_loop(SECOND_AT, THIRD_AT, stencil, 0)
    gram_third()
    lax.fori_loop(THIRD_AT, N_X - 1, stencil, 0)
    arrive(N_X - 1)
    ship_past()
    lax.fori_loop(N_X - 1, N_X, advance, 0)

    fold_fresh(sums_ref, fresh)

    def pick_fresh(step, carry):
        fresh_ship[step] = fresh[piece_of(owner, lax.rem(group + step, N_GROUP))]
        return carry

    lax.fori_loop(0, N_GROUP, pick_fresh, 0)
    fresh_in[group] = fresh_ship[0]
    broadcast(
        "group", N_GROUP, lambda step: fresh_ship.at[step], fresh_in.at[group], piece_send.at[1], piece_recv.at[1]
    )

    drain(full.at[pl.ds(0, N_WALL - 1)], sum_recv.at[2])
    matrix[...] = full[...].reshape(RANK, RANK)
    invert(matrix, 0, SWEPT[0])

    drain(ship.at[pl.ds(0, N_GROUP - 1)], piece_recv.at[0])
    drain(fresh_ship.at[pl.ds(0, N_GROUP - 1)], piece_recv.at[1])
    last = lax.broadcasted_iota(jnp.int32, (COUNT, LANES), 0) == COUNT - 1
    for plane in range(PLANES):
        for h in range(N_GROUP):
            start = (plane * N_GROUP + h) * LANES
            sheet[:, start : start + LANES] = jnp.where(
                last, fresh_in[h, plane : plane + 1, :], rows[plane, h]
            )

    def project(step, total):
        head, tail = split(sheet[:, lanes_of(step)])
        both = dot(top[step], jnp.concatenate([head, tail], axis=0), NT)
        return total + both[:, :COUNT] + both[:, COUNT:] + dot(rest[step], head, NT)

    proj = lax.fori_loop(0, N_CHUNK, project, jnp.zeros((RANK, COUNT), F32), unroll=12).T

    def sum_first(value, pole_ref, place):
        pole = pole_index()
        pole_ref[pole] = value
        broadcast(
            "pole", N_POLE, lambda step: pole_ref.at[pole], pole_ref.at[pole],
            sum_send.at[place], sum_recv.at[place],
        )

    def sum_second(pole_ref, plane_ref, place):
        drain(pole_ref.at[pl.ds(0, N_POLE - 1)], sum_recv.at[place])
        plane = plane_index()
        plane_ref[plane] = add_slots(pole_ref)
        broadcast(
            "plane", N_PLANE, lambda step: plane_ref.at[plane], plane_ref.at[plane],
            sum_send.at[place + 1], sum_recv.at[place + 1],
        )

    def sum_end(plane_ref, place):
        drain(plane_ref.at[pl.ds(0, N_PLANE - 1)], sum_recv.at[place + 1])
        return add_slots(plane_ref) * (1.0 / (ROWS * N_GROUP * N_SLAB))

    sum_first(proj, proj_pole, 3)
    invert(matrix, SWEPT[0], SWEPT[1])
    sum_second(proj_pole, proj_plane, 3)
    invert(matrix, SWEPT[1], RANK // BLOCK)
    proj = sum_end(proj_plane, 3)
    solved = -dot(proj, matrix[...], NN, HIGH)
    weights[...] = solved

    head, tail = split(solved)
    both_parts = jnp.concatenate([head, tail], axis=0)

    def subtract(step, total):
        both = dot(both_parts, top[step], NN)
        image = both[:COUNT] + both[COUNT:] + dot(head, rest[step], NN)
        part = sheet[:, lanes_of(step)] - image
        sheet[:, lanes_of(step)] = part
        return total + dot(part, part, NT, HIGH)

    inner = lax.fori_loop(0, N_CHUNK, subtract, jnp.zeros((COUNT, COUNT), F32), unroll=12)
    sum_first(jnp.concatenate([inner, jnp.zeros((COUNT, 128 - COUNT), F32)], axis=1), res_pole, 5)

    def finish(chunk, carry):
        for which in range(2):
            halo(chunk, which).wait_send()
        return carry

    lax.fori_loop(0, N_X, finish, 0)
    drain(ship.at[pl.ds(0, N_GROUP - 1)], piece_send.at[0])
    drain(fresh_ship.at[pl.ds(0, N_GROUP - 1)], piece_send.at[1])
    drain(shares.at[pl.ds(0, N_WALL - 1)], sum_send.at[0])
    drain(rings.at[pl.ds(0, N_RING - 1)], sum_send.at[1])
    drain(full.at[pl.ds(0, N_WALL - 1)], sum_send.at[2])
    drain(proj_pole.at[pl.ds(0, N_POLE - 1)], sum_send.at[3])
    drain(proj_plane.at[pl.ds(0, N_PLANE - 1)], sum_send.at[4])
    sum_second(res_pole, res_plane, 5)
    drain(res_pole.at[pl.ds(0, N_POLE - 1)], sum_send.at[5])
    wgram[...] = sum_end(res_plane, 5)
    drain(res_plane.at[pl.ds(0, N_PLANE - 1)], sum_send.at[6])


FIRST, AHEAD = 3, 4
GRAM_FIRST = 3
SECOND_AT, THIRD_AT = 3, 6
SWEPT = (3, 5)


def section(velocity, register, basis, past, owner):
    hbm = pl.BlockSpec(memory_space=pltpu.HBM)
    vmem = pl.BlockSpec(memory_space=pltpu.VMEM)
    dma = pltpu.SemaphoreType.DMA
    field = (3, 128, 16, 128)
    face = (3, 128, reach, 128)
    pieces = (N_GROUP, PLANES, COUNT, LANES)
    fresh = (N_GROUP, PLANES, LANES)
    scratch = [
        (field, F32), (face, F32), (face, F32), (face, F32), (face, F32),
        ((N_CHUNK, RANK, CHUNK), F32), ((N_CHUNK, RANK, CHUNK), BF16), ((N_CHUNK, RANK, CHUNK), BF16),
        ((COUNT - 1, PLANES, 32, 96), F32), (pieces, F32), (pieces, F32), ((PLANES, N_GROUP, COUNT, LANES), F32),
        ((RANK, 2 * RANK), F32), ((N_WALL, BAND, RANK), F32), ((N_WALL, BAND, RANK), F32),
        ((N_RING, BAND, RANK), F32), ((BAND, RANK), F32), ((N_WALL, BAND, RANK), F32), ((RANK, RANK), F32),
        ((1536, 128), F32), (fresh, F32), (fresh, F32), (fresh, F32),
        ((N_POLE, COUNT, RANK), F32), ((N_PLANE, COUNT, RANK), F32),
        ((N_POLE, COUNT, 128), F32), ((N_PLANE, COUNT, 128), F32),
    ]
    semaphores = [(N_X,), (N_X,), (2, N_X), (2, N_X), (N_CHUNK,), None, (2,), (2,), (7,), (7,)]
    return pl.pallas_call(
        section_kernel,
        in_specs=[hbm] * 4 + [pl.BlockSpec(memory_space=pltpu.SMEM)],
        out_specs=[vmem] * 5,
        out_shape=[
            pltpu.VMEM(shape, F32)
            for shape in (field, field, (COUNT, RANK), (COUNT, 128), (COUNT, ROWS))
        ],
        scratch_shapes=[pltpu.VMEM(shape, kind) for shape, kind in scratch]
        + [dma if shape is None else dma(shape) for shape in semaphores],
        compiler_params=pltpu.CompilerParams(
            collective_id=0, has_side_effects=True, vmem_limit_bytes=46 * MIB
        ),
        name="section",
    )(velocity, register, basis, past, owner)


def finish_kernel(new_v, reg, weights, wgram_ref, residual, out_v, out_r, coeffs, factor, out_d, directions, sems, last_sem):
    copies = [
        pltpu.make_async_copy(source.at[c], target.at[c], sems.at[which, c])
        for which, (source, target) in enumerate(((new_v, out_v), (reg, out_r)))
        for c in range(3)
    ]
    for copy in copies:
        copy.start()
    coeffs[...] = weights[...]
    wgram = wgram_ref[...]
    lane = lax.broadcasted_iota(jnp.int32, (COUNT, 128), 1)
    row = lax.broadcasted_iota(jnp.int32, (COUNT, 128), 0)
    lower = jnp.zeros((COUNT, 128), F32)
    inverse = jnp.where(lane == row, 1.0, 0.0)
    for q in range(COUNT):
        scale = lax.rsqrt(wgram[q : q + 1, q : q + 1])
        column = wgram[:, q : q + 1] * scale
        column = jnp.where(row[:, :1] >= q, column, 0.0)
        lower = jnp.where(lane == q, column, lower)
        line = wgram[q : q + 1, :] * scale
        below = jnp.where(row[:, :1] > q, column, 0.0)
        wgram = wgram - below * line
        solved = inverse[q : q + 1, :] * scale
        inverse = jnp.where(row == q, solved, inverse - below * solved)
    factor[...] = lower[:, :COUNT]
    columns = [inverse[:, q : q + 1] for q in range(COUNT)]

    def direct(step, carry):
        lanes = pl.ds(pl.multiple_of(step * CHUNK, CHUNK), CHUNK)
        part = residual[:, lanes]
        total = columns[0] * part[0:1, :]
        for q in range(1, COUNT):
            total = total + columns[q] * part[q : q + 1, :]
        directions[:, lanes] = total
        return carry

    lax.fori_loop(0, N_CHUNK, direct, 0)
    copies.append(pltpu.make_async_copy(directions, out_d, last_sem))
    copies[-1].start()
    for copy in copies:
        copy.wait()


def finish(*operands):
    operands = [pltpu.with_memory_space_constraint(operand, pltpu.VMEM) for operand in operands]
    vmem = pl.BlockSpec(memory_space=pltpu.VMEM)
    hbm = pl.BlockSpec(memory_space=pltpu.HBM)
    return pl.pallas_call(
        finish_kernel,
        out_shape=[
            jax.ShapeDtypeStruct((3, 128, 16, 128), F32),
            jax.ShapeDtypeStruct((3, 128, 16, 128), F32),
            jax.ShapeDtypeStruct((COUNT, RANK), F32),
            jax.ShapeDtypeStruct((COUNT, COUNT), F32),
            jax.ShapeDtypeStruct((COUNT, ROWS), F32),
        ],
        in_specs=[vmem] * 5,
        out_specs=[hbm, hbm, vmem, vmem, hbm],
        scratch_shapes=[
            pltpu.VMEM((COUNT, ROWS), F32),
            pltpu.SemaphoreType.DMA((2, 3)),
            pltpu.SemaphoreType.DMA,
        ],
        compiler_params=pltpu.CompilerParams(vmem_limit_bytes=8 * MIB),
        name="finish",
    )(*operands)


def local(velocity, register, past, basis, owner):
    operands = section(
        velocity.transpose(0, 1, 3, 2),
        register.transpose(0, 1, 3, 2),
        basis.reshape(RANK, ROWS),
        pltpu.with_memory_space_constraint(past, pltpu.HBM),
        pltpu.with_memory_space_constraint(owner.T, pltpu.HBM),
    )
    new_v, new_r, coeffs, factor, directions = finish(*operands)
    return (
        new_v.transpose(0, 1, 3, 2),
        new_r.transpose(0, 1, 3, 2),
        coeffs.T,
        factor,
        directions.reshape(1, 1, COUNT, ROWS),
    )


def solution(mesh):
    in_specs = (
        P(None, None, None, ("group", "slab")),
        P(None, None, None, ("group", "slab")),
        P(None, ("group", "slab"), None, None),
        P("slab", "group", None, None),
        P(),
    )
    out_specs = (
        P(None, None, None, ("group", "slab")),
        P(None, None, None, ("group", "slab")),
        P(),
        P(),
        P("slab", "group", None, None),
    )
    return jax.shard_map(local, mesh=mesh, in_specs=in_specs, out_specs=out_specs, check_vma=False)
```

```python
import functools

import jax
import jax.numpy as jnp
from jax import lax
from jax.experimental import pallas as pl
from jax.experimental.pallas import tpu as pltpu
from jax.sharding import PartitionSpec as P

first_coef = (0.8, -0.2, 4.0 / 105.0, -1.0 / 280.0)
second_coef = (-205.0 / 72.0, 1.6, -0.2, 8.0 / 315.0, -1.0 / 560.0)
time_step = 0.02
viscosity = 0.4
section_decay = -5.0 / 9.0
section_gain = 15.0 / 16.0
reach = 4

F32 = jnp.float32
BF16 = jnp.bfloat16
HIGH = lax.Precision.HIGHEST
NT = (((1,), (1,)), ((), ()))
TN = (((0,), (0,)), ((), ()))
NN = (((1,), (0,)), ((), ()))
N_GROUP = 8
N_SLAB = 16
N_POLE = 8
N_PLANE = 16
N_WALL = 32
N_RING = 4
RANK = 256
ROWS = 12288
COUNT = 8
PLANES = 4
LANES = 384
CHUNK = 1024
N_CHUNK = ROWS // CHUNK
BAND = RANK // N_WALL
X_CHUNK = 16
N_X = 128 // X_CHUNK
BLOCK = 32
MIB = 2**20


def dot(left, right, dims, precision=None):
    return lax.dot_general(
        left, right, dims, precision=precision, preferred_element_type=F32
    )


def split(value):
    high = value.astype(BF16)
    return high, (value - high.astype(F32)).astype(BF16)


def in_parts(value):
    high, rest = value.astype(BF16), value - value.astype(BF16).astype(F32)
    middle = rest.astype(BF16)
    return high, middle, (rest - middle.astype(F32)).astype(BF16)


def product(left, right, dims):
    (a, b, c), (d, e, f) = in_parts(left), in_parts(right)
    (over_left,), (over_right,) = dims[0]
    return dot(
        jnp.concatenate([a, a, b, b, a, c], axis=over_left),
        jnp.concatenate([d, e, d, e, f, d], axis=over_right),
        dims,
    )


def peer(axis, step):
    group, slab = lax.axis_index("group"), lax.axis_index("slab")
    if axis == "group":
        return (lax.rem(group + step, N_GROUP), slab)
    column = lax.rem(slab // 2, 2)
    if axis == "wall":
        place = lax.rem(wall_index() + step, N_WALL)
        within = lax.rem(place, N_POLE)
        return (group // 4 * 4 + place // N_POLE, within // 2 * 4 + column * 2 + lax.rem(within, 2))
    if axis == "ring":
        place = lax.rem(ring_index() + step, N_RING)
        return (place // 2 * 4 + lax.rem(group, 4), slab - column * 2 + lax.rem(place, 2) * 2)
    if axis == "pole":
        place = lax.rem(pole_index() + step, N_POLE)
        return (group, place // 2 * 4 + column * 2 + lax.rem(place, 2))
    place = lax.rem(plane_index() + step, N_PLANE)
    return (place // 2, slab - column * 2 + lax.rem(place, 2) * 2)


def pole_index():
    slab = lax.axis_index("slab")
    return slab // 4 * 2 + lax.rem(slab, 2)


def wall_index():
    return lax.rem(lax.axis_index("group"), 4) * N_POLE + pole_index()


def ring_index():
    return lax.axis_index("group") // 4 * 2 + lax.rem(lax.axis_index("slab") // 2, 2)


def plane_index():
    return lax.axis_index("group") * 2 + lax.rem(lax.axis_index("slab") // 2, 2)


def linear(step):
    total = N_GROUP * N_SLAB
    place = lax.rem(lax.axis_index("group") * N_SLAB + lax.axis_index("slab") + step + total, total)
    return (place // N_SLAB, lax.rem(place, N_SLAB))


def hello():
    barrier = pltpu.get_barrier_semaphore()
    for axis, size in (("plane", N_PLANE), ("wall", N_WALL)):

        def signal(step, carry, axis=axis):
            pl.semaphore_signal(barrier, inc=1, device_id=peer(axis, step))
            return carry

        lax.fori_loop(1, size, signal, 0)
    for step in (1, -1):
        pl.semaphore_signal(barrier, inc=1, device_id=linear(step))


def everyone_in():
    pl.semaphore_wait(pltpu.get_barrier_semaphore(), N_WALL + N_PLANE)


def broadcast(axis, size, source, target, send_sem, recv_sem):
    def send(step, carry):
        pltpu.make_async_remote_copy(
            src_ref=source(step),
            dst_ref=target,
            send_sem=send_sem,
            recv_sem=recv_sem,
            device_id=peer(axis, step),
        ).start()
        return carry

    lax.fori_loop(1, size, send, 0)


def drain(ref, *sems):
    for sem in sems:
        pltpu.make_async_copy(ref, ref, sem).wait()


def add_slots(ref):
    total = ref[0]
    for slot in range(1, ref.shape[0]):
        total = total + ref[slot]
    return total


def piece_of(owner, group):
    slab = lax.axis_index("slab")
    place = jnp.int32(0)
    for piece in range(N_GROUP):
        place = jnp.where(owner[piece, slab] == group, piece, place)
    return place


def sweep_block(block):
    lane = lax.broadcasted_iota(jnp.int32, (8, 128), 1)
    row = lax.broadcasted_iota(jnp.int32, (8, 128), 0)
    count = block.shape[0] // 8
    parts = [block[8 * i : 8 * i + 8] for i in range(count)]
    for b in range(count):
        line = parts[b]
        columns = [jnp.broadcast_to(line[:, 8 * b + j : 8 * b + j + 1], (8, 128)) for j in range(8)]
        inside = (lane >= 8 * b) & (lane < 8 * b + 8)
        line = jnp.where(inside, jnp.where(lane - 8 * b == row, -1.0, 0.0), line)
        for q in range(8):
            pivot = 1.0 / columns[q][q : q + 1, :]
            solved = line[q : q + 1, :] * pivot
            others = jnp.where(row == q, 0.0, columns[q])
            line = jnp.where(row == q, solved, line - others * solved)
            for j in range(q + 1, 8):
                entry = columns[j][q : q + 1, :] * pivot
                columns[j] = jnp.where(row == q, entry, columns[j] - others * entry)
        for i in range(count):
            if i != b:
                part = parts[i]
                total = jnp.where(inside, 0.0, part)
                for j in range(8):
                    column = jnp.broadcast_to(part[:, 8 * b + j : 8 * b + j + 1], (8, 128))
                    total = total - column * line[j : j + 1, :]
                parts[i] = total
        parts[b] = line
    return -jnp.concatenate(parts, axis=0)


def invert(matrix, first, last):
    lane = lax.broadcasted_iota(jnp.int32, (BLOCK, RANK), 1)
    row = lax.broadcasted_iota(jnp.int32, (BLOCK, RANK), 0)
    wide = lax.broadcasted_iota(jnp.int32, (RANK, RANK), 1)
    for k in range(first, last):
        start = k * BLOCK
        panel = matrix[start : start + BLOCK, :]
        tile = start // 128 * 128
        diagonal = panel[:, tile : tile + 128]
        if start % 128:
            diagonal = pltpu.roll(diagonal, 128 - start % 128, 1)
        inverse = sweep_block(diagonal)[:, :BLOCK]
        inside = (lane >= start) & (lane < start + BLOCK)
        eye = jnp.where(lane - start == row, -1.0, 0.0)
        solved = product(inverse, jnp.where(inside, eye, panel), NN)
        inside = (wide >= start) & (wide < start + BLOCK)
        matrix[...] = jnp.where(inside, 0.0, matrix[...]) - product(panel, solved, TN)
        matrix[start : start + BLOCK, :] = solved


def fold_fresh(sums_ref, fresh):
    rows = sums_ref[pl.ds(0, 384, 4), :]
    for z in range(1, 4):
        rows = rows + sums_ref[pl.ds(z, 384, 4), :]
    row = lax.broadcasted_iota(jnp.int32, (512, 128), 0)
    lane = lax.broadcasted_iota(jnp.int32, (512, 128), 1)
    fold = jnp.where((row // 128 == lane // 32) & ((row % 128) // 4 == lane % 32), 1 / 64, 0.0).astype(BF16)
    tiles = []
    for tile in range(3):
        parts = []
        for m in range(4):
            j, c = divmod(4 * tile + m, 3)
            parts.append(rows[(c * 4 + j) * 32 : (c * 4 + j) * 32 + 32])
        tiles.append(jnp.concatenate(parts, axis=1))
    boxes = jnp.concatenate(tiles, axis=0)
    means = dot(jnp.concatenate(in_parts(boxes), axis=0), fold, NN)
    means = means[:96] + (means[96:192] + means[192:])
    for tile in range(3):
        part = means[tile * 32 : (tile + 1) * 32]
        fresh[:, :, tile * 128 : (tile + 1) * 128] = part.reshape(N_GROUP, PLANES, 128)


def column(v, low, high, register, new_v, x):
    center = [v[c, x] for c in range(3)]
    coef = []
    for axis in range(3):
        row = []
        for k in range(4):
            drift = center[axis] * first_coef[k]
            diffuse = viscosity * second_coef[k + 1]
            row.append((diffuse - drift, diffuse + drift))
        coef.append(row)
    outs = []
    for c in range(3):
        tall = jnp.concatenate([low[c, x], center[c], high[c, x]], axis=0)
        total = center[c] * (3.0 * viscosity * second_coef[0])
        for k in range(1, 5):
            up, down = coef[0][k - 1]
            total = total + v[c, (x + k) & 127] * up + v[c, (x - k) & 127] * down
        for k in range(1, 5):
            up, down = coef[1][k - 1]
            total = total + pltpu.roll(center[c], 128 - k, 1) * up
            total = total + pltpu.roll(center[c], k, 1) * down
        for k in range(1, 5):
            up, down = coef[2][k - 1]
            total = total + tall[reach + k : reach + k + 16] * up
            total = total + tall[reach - k : reach - k + 16] * down
        moved = register[c, x] * section_decay + time_step * total
        register[c, x] = moved
        fluid = center[c] + section_gain * moved
        new_v[c, x] = fluid
        outs.append(fluid)
    return outs


def section_kernel(
    velocity, register, basis, past, owner,
    new_v, reg, weights, wgram, sheet,
    field, edge_low, edge_high, low, high, blocks, top, rest, past_v, pieces, ship, rows,
    local, partial, shares, rings, band, full, matrix, sums_ref, fresh, fresh_ship, fresh_in,
    proj_pole, proj_plane, res_pole, res_plane,
    field_sem, reg_sem, halo_send, halo_recv, block_sem, past_sem, piece_send, piece_recv, sum_send, sum_recv,
):
    group = lax.axis_index("group")

    def part_of(chunk):
        return pl.ds(pl.multiple_of(chunk * X_CHUNK, X_CHUNK), X_CHUNK)

    def lanes_of(step):
        return pl.ds(pl.multiple_of(step * CHUNK, CHUNK), CHUNK)

    def field_load(chunk):
        part = part_of(chunk)
        return pltpu.make_async_copy(velocity.at[:, part], field.at[:, part], field_sem.at[chunk])

    def reg_load(chunk):
        part = part_of(chunk)
        return pltpu.make_async_copy(register.at[:, part], reg.at[:, part], reg_sem.at[chunk])

    def block_load(step):
        return pltpu.make_async_copy(basis.at[:, lanes_of(step)], blocks.at[step], block_sem.at[step])

    def start_each(count, make):
        def begin(step, carry):
            make(step).start()
            return carry

        lax.fori_loop(0, count, begin, 0)

    start_each(N_X, field_load)
    hello()
    past_load = pltpu.make_async_copy(past, past_v, past_sem)
    start_each(N_CHUNK, block_load)
    past_load.start()
    start_each(N_X, reg_load)

    def halo(chunk, side):
        part = part_of(chunk)
        edge, target = ((edge_high, low), (edge_low, high))[side]
        return pltpu.make_async_remote_copy(
            src_ref=edge.at[:, part],
            dst_ref=target.at[:, part],
            send_sem=halo_send.at[side, chunk],
            recv_sem=halo_recv.at[side, chunk],
            device_id=linear((1, -1)[side]),
        )

    def face(chunk, carry):
        field_load(chunk).wait()
        part = part_of(chunk)
        edge_low[:, part] = field[:, part, 0:reach, :]
        edge_high[:, part] = field[:, part, 16 - reach : 16, :]
        return carry

    def face_send(chunk, carry):
        halo(chunk, 0).start()
        halo(chunk, 1).start()
        return carry

    lax.fori_loop(0, N_X, face, 0)

    local[...] = jnp.zeros_like(local)

    def multiply(step, carry):
        block_load(step).wait()
        upper, lower = split(blocks[step])
        top[step], rest[step] = upper, lower
        local[...] += dot(upper, jnp.concatenate([upper, lower], axis=0), NT)
        return carry

    lax.fori_loop(0, GRAM_FIRST, multiply, 0)
    everyone_in()
    lax.fori_loop(0, FIRST, face_send, 0)
    lax.fori_loop(GRAM_FIRST, N_CHUNK, multiply, 0)
    cross = local[:, RANK:]
    partial[...] = (local[:, :RANK] + cross + cross.T).reshape(N_WALL, BAND, RANK)

    wall, ring = wall_index(), ring_index()

    def gram_first():
        broadcast(
            "wall", N_WALL, lambda step: partial.at[lax.rem(wall + step, N_WALL)], shares.at[wall],
            sum_send.at[0], sum_recv.at[0],
        )
        shares[wall] = partial[wall]

    def gram_second():
        drain(shares.at[pl.ds(0, N_WALL - 1)], sum_recv.at[0])
        rings[ring] = add_slots(shares)
        broadcast(
            "ring", N_RING, lambda step: rings.at[ring], rings.at[ring], sum_send.at[1], sum_recv.at[1]
        )

    def gram_third():
        drain(rings.at[pl.ds(0, N_RING - 1)], sum_recv.at[1])
        band[...] = add_slots(rings) * (1.0 / (ROWS * N_GROUP * N_SLAB))
        full[wall] = band[...]
        broadcast("wall", N_WALL, lambda step: band, full.at[wall], sum_send.at[2], sum_recv.at[2])

    gram_first()
    lax.fori_loop(FIRST, AHEAD, face_send, 0)

    past_load.wait()
    pieces[...] = jnp.zeros_like(pieces)

    def arrange(place, carry):
        piece, plane = place // PLANES, lax.rem(place, PLANES)
        parts = [past_v[:, plane, pl.ds(piece * 4 + j, 1), :].reshape(COUNT - 1, 96) for j in range(4)]
        pieces[piece, plane, 0 : COUNT - 1, :] = jnp.concatenate(parts, axis=1)
        return carry

    lax.fori_loop(0, N_GROUP * PLANES, arrange, 0)

    def pick(step, carry):
        ship[step] = pieces[piece_of(owner, lax.rem(group + step, N_GROUP))]
        return carry

    lax.fori_loop(0, N_GROUP, pick, 0)
    rows[:, group] = ship[0]

    def ship_past():
        broadcast(
            "group", N_GROUP, lambda step: ship.at[step], rows.at[:, group], piece_send.at[0], piece_recv.at[0]
        )

    def arrive(chunk):
        halo(chunk, 0).wait_recv()
        halo(chunk, 1).wait_recv()
        reg_load(chunk).wait()

    def stencil(chunk, carry):
        arrive(chunk)
        return advance(chunk, carry)

    def advance(chunk, carry):

        @pl.when(chunk + AHEAD < N_X)
        def _():
            face_send(chunk + AHEAD, 0)

        def coarse(quad, carry):
            x = chunk * X_CHUNK + quad * 4
            sums = column(field, low, high, reg, new_v, x)
            for j in range(1, 4):
                sums = [a + b for a, b in zip(sums, column(field, low, high, reg, new_v, x + j))]
            across = chunk * (X_CHUNK // 4) + quad
            j, piece = lax.rem(across, 4), across // 4
            for c in range(3):
                place = ((c * 4 + j) * N_GROUP + piece) * 16
                sums_ref[pl.ds(pl.multiple_of(place, 16), 16), :] = sums[c]
            return carry

        lax.fori_loop(0, X_CHUNK // 4, coarse, 0)
        return carry

    lax.fori_loop(0, SECOND_AT, stencil, 0)
    gram_second()
    lax.fori_loop(SECOND_AT, THIRD_AT, stencil, 0)
    gram_third()
    lax.fori_loop(THIRD_AT, N_X - 1, stencil, 0)
    arrive(N_X - 1)
    ship_past()
    lax.fori_loop(N_X - 1, N_X, advance, 0)

    fold_fresh(sums_ref, fresh)

    def pick_fresh(step, carry):
        fresh_ship[step] = fresh[piece_of(owner, lax.rem(group + step, N_GROUP))]
        return carry

    lax.fori_loop(0, N_GROUP, pick_fresh, 0)
    fresh_in[group] = fresh_ship[0]
    broadcast(
        "group", N_GROUP, lambda step: fresh_ship.at[step], fresh_in.at[group], piece_send.at[1], piece_recv.at[1]
    )

    drain(full.at[pl.ds(0, N_WALL - 1)], sum_recv.at[2])
    matrix[...] = full[...].reshape(RANK, RANK)
    invert(matrix, 0, SWEPT[0])

    drain(ship.at[pl.ds(0, N_GROUP - 1)], piece_recv.at[0])
    drain(fresh_ship.at[pl.ds(0, N_GROUP - 1)], piece_recv.at[1])
    last = lax.broadcasted_iota(jnp.int32, (COUNT, LANES), 0) == COUNT - 1
    for plane in range(PLANES):
        for h in range(N_GROUP):
            start = (plane * N_GROUP + h) * LANES
            sheet[:, start : start + LANES] = jnp.where(
                last, fresh_in[h, plane : plane + 1, :], rows[plane, h]
            )

    def project(step, total):
        head, tail = split(sheet[:, lanes_of(step)])
        both = dot(top[step], jnp.concatenate([head, tail], axis=0), NT)
        return total + both[:, :COUNT] + both[:, COUNT:] + dot(rest[step], head, NT)

    proj = lax.fori_loop(0, N_CHUNK, project, jnp.zeros((RANK, COUNT), F32), unroll=12).T

    def sum_first(value, pole_ref, place):
        pole = pole_index()
        pole_ref[pole] = value
        broadcast(
            "pole", N_POLE, lambda step: pole_ref.at[pole], pole_ref.at[pole],
            sum_send.at[place], sum_recv.at[place],
        )

    def sum_second(pole_ref, plane_ref, place):
        drain(pole_ref.at[pl.ds(0, N_POLE - 1)], sum_recv.at[place])
        plane = plane_index()
        plane_ref[plane] = add_slots(pole_ref)
        broadcast(
            "plane", N_PLANE, lambda step: plane_ref.at[plane], plane_ref.at[plane],
            sum_send.at[place + 1], sum_recv.at[place + 1],
        )

    def sum_end(plane_ref, place):
        drain(plane_ref.at[pl.ds(0, N_PLANE - 1)], sum_recv.at[place + 1])
        return add_slots(plane_ref) * (1.0 / (ROWS * N_GROUP * N_SLAB))

    sum_first(proj, proj_pole, 3)
    invert(matrix, SWEPT[0], SWEPT[1])
    sum_second(proj_pole, proj_plane, 3)
    invert(matrix, SWEPT[1], RANK // BLOCK)
    proj = sum_end(proj_plane, 3)
    solved = -dot(proj, matrix[...], NN, HIGH)
    weights[...] = solved

    head, tail = split(solved)
    both_parts = jnp.concatenate([head, tail], axis=0)

    def subtract(step, total):
        both = dot(both_parts, top[step], NN)
        image = both[:COUNT] + both[COUNT:] + dot(head, rest[step], NN)
        part = sheet[:, lanes_of(step)] - image
        sheet[:, lanes_of(step)] = part
        return total

    lax.fori_loop(0, N_CHUNK, subtract, 0, unroll=12)
    residual = sheet[...]
    inner = dot(residual, residual, NT, HIGH)
    sum_first(jnp.concatenate([inner, jnp.zeros((COUNT, 128 - COUNT), F32)], axis=1), res_pole, 5)

    def finish(chunk, carry):
        for which in range(2):
            halo(chunk, which).wait_send()
        return carry

    lax.fori_loop(0, N_X, finish, 0)
    drain(ship.at[pl.ds(0, N_GROUP - 1)], piece_send.at[0])
    drain(fresh_ship.at[pl.ds(0, N_GROUP - 1)], piece_send.at[1])
    drain(shares.at[pl.ds(0, N_WALL - 1)], sum_send.at[0])
    drain(rings.at[pl.ds(0, N_RING - 1)], sum_send.at[1])
    drain(full.at[pl.ds(0, N_WALL - 1)], sum_send.at[2])
    drain(proj_pole.at[pl.ds(0, N_POLE - 1)], sum_send.at[3])
    drain(proj_plane.at[pl.ds(0, N_PLANE - 1)], sum_send.at[4])
    sum_second(res_pole, res_plane, 5)
    drain(res_pole.at[pl.ds(0, N_POLE - 1)], sum_send.at[5])
    wgram[...] = sum_end(res_plane, 5)
    drain(res_plane.at[pl.ds(0, N_PLANE - 1)], sum_send.at[6])


FIRST, AHEAD = 3, 4
GRAM_FIRST = 4
SECOND_AT, THIRD_AT = 3, 5
SWEPT = (3, 5)


def section(velocity, register, basis, past, owner):
    hbm = pl.BlockSpec(memory_space=pltpu.HBM)
    vmem = pl.BlockSpec(memory_space=pltpu.VMEM)
    dma = pltpu.SemaphoreType.DMA
    field = (3, 128, 16, 128)
    face = (3, 128, reach, 128)
    pieces = (N_GROUP, PLANES, COUNT, LANES)
    fresh = (N_GROUP, PLANES, LANES)
    scratch = [
        (field, F32), (face, F32), (face, F32), (face, F32), (face, F32),
        ((N_CHUNK, RANK, CHUNK), F32), ((N_CHUNK, RANK, CHUNK), BF16), ((N_CHUNK, RANK, CHUNK), BF16),
        ((COUNT - 1, PLANES, 32, 96), F32), (pieces, F32), (pieces, F32), ((PLANES, N_GROUP, COUNT, LANES), F32),
        ((RANK, 2 * RANK), F32), ((N_WALL, BAND, RANK), F32), ((N_WALL, BAND, RANK), F32),
        ((N_RING, BAND, RANK), F32), ((BAND, RANK), F32), ((N_WALL, BAND, RANK), F32), ((RANK, RANK), F32),
        ((1536, 128), F32), (fresh, F32), (fresh, F32), (fresh, F32),
        ((N_POLE, COUNT, RANK), F32), ((N_PLANE, COUNT, RANK), F32),
        ((N_POLE, COUNT, 128), F32), ((N_PLANE, COUNT, 128), F32),
    ]
    semaphores = [(N_X,), (N_X,), (2, N_X), (2, N_X), (N_CHUNK,), None, (2,), (2,), (7,), (7,)]
    return pl.pallas_call(
        section_kernel,
        in_specs=[hbm] * 4 + [pl.BlockSpec(memory_space=pltpu.SMEM)],
        out_specs=[vmem] * 5,
        out_shape=[
            pltpu.VMEM(shape, F32)
            for shape in (field, field, (COUNT, RANK), (COUNT, 128), (COUNT, ROWS))
        ],
        scratch_shapes=[pltpu.VMEM(shape, kind) for shape, kind in scratch]
        + [dma if shape is None else dma(shape) for shape in semaphores],
        compiler_params=pltpu.CompilerParams(
            collective_id=0, has_side_effects=True, vmem_limit_bytes=46 * MIB
        ),
        name="section",
    )(velocity, register, basis, past, owner)


def finish_kernel(new_v, reg, weights, wgram_ref, residual, out_v, out_r, coeffs, factor, out_d, directions, sems, last_sem):
    copies = [
        pltpu.make_async_copy(source.at[c], target.at[c], sems.at[which, c])
        for which, (source, target) in enumerate(((new_v, out_v), (reg, out_r)))
        for c in range(3)
    ]
    for copy in copies:
        copy.start()
    coeffs[...] = weights[...]
    wgram = wgram_ref[...]
    lane = lax.broadcasted_iota(jnp.int32, (COUNT, 128), 1)
    row = lax.broadcasted_iota(jnp.int32, (COUNT, 128), 0)
    lower = jnp.zeros((COUNT, 128), F32)
    inverse = jnp.where(lane == row, 1.0, 0.0)
    for q in range(COUNT):
        scale = lax.rsqrt(wgram[q : q + 1, q : q + 1])
        column = wgram[:, q : q + 1] * scale
        column = jnp.where(row[:, :1] >= q, column, 0.0)
        lower = jnp.where(lane == q, column, lower)
        line = wgram[q : q + 1, :] * scale
        below = jnp.where(row[:, :1] > q, column, 0.0)
        wgram = wgram - below * line
        solved = inverse[q : q + 1, :] * scale
        inverse = jnp.where(row == q, solved, inverse - below * solved)
    factor[...] = lower[:, :COUNT]
    columns = [inverse[:, q : q + 1] for q in range(COUNT)]

    def direct(step, carry):
        lanes = pl.ds(pl.multiple_of(step * CHUNK, CHUNK), CHUNK)
        part = residual[:, lanes]
        total = columns[0] * part[0:1, :]
        for q in range(1, COUNT):
            total = total + columns[q] * part[q : q + 1, :]
        directions[:, lanes] = total
        return carry

    lax.fori_loop(0, N_CHUNK, direct, 0)
    copies.append(pltpu.make_async_copy(directions, out_d, last_sem))
    copies[-1].start()
    for copy in copies:
        copy.wait()


def finish(*operands):
    operands = [pltpu.with_memory_space_constraint(operand, pltpu.VMEM) for operand in operands]
    vmem = pl.BlockSpec(memory_space=pltpu.VMEM)
    hbm = pl.BlockSpec(memory_space=pltpu.HBM)
    return pl.pallas_call(
        finish_kernel,
        out_shape=[
            jax.ShapeDtypeStruct((3, 128, 16, 128), F32),
            jax.ShapeDtypeStruct((3, 128, 16, 128), F32),
            jax.ShapeDtypeStruct((COUNT, RANK), F32),
            jax.ShapeDtypeStruct((COUNT, COUNT), F32),
            jax.ShapeDtypeStruct((COUNT, ROWS), F32),
        ],
        in_specs=[vmem] * 5,
        out_specs=[hbm, hbm, vmem, vmem, hbm],
        scratch_shapes=[
            pltpu.VMEM((COUNT, ROWS), F32),
            pltpu.SemaphoreType.DMA((2, 3)),
            pltpu.SemaphoreType.DMA,
        ],
        compiler_params=pltpu.CompilerParams(vmem_limit_bytes=8 * MIB),
        name="finish",
    )(*operands)


def local(velocity, register, past, basis, owner):
    operands = section(
        velocity.transpose(0, 1, 3, 2),
        register.transpose(0, 1, 3, 2),
        basis.reshape(RANK, ROWS),
        pltpu.with_memory_space_constraint(past, pltpu.HBM),
        pltpu.with_memory_space_constraint(owner.T, pltpu.HBM),
    )
    new_v, new_r, coeffs, factor, directions = finish(*operands)
    return (
        new_v.transpose(0, 1, 3, 2),
        new_r.transpose(0, 1, 3, 2),
        coeffs.T,
        factor,
        directions.reshape(1, 1, COUNT, ROWS),
    )


def solution(mesh):
    in_specs = (
        P(None, None, None, ("group", "slab")),
        P(None, None, None, ("group", "slab")),
        P(None, ("group", "slab"), None, None),
        P("slab", "group", None, None),
        P(),
    )
    out_specs = (
        P(None, None, None, ("group", "slab")),
        P(None, None, None, ("group", "slab")),
        P(),
        P(),
        P("slab", "group", None, None),
    )
    return jax.shard_map(local, mesh=mesh, in_specs=in_specs, out_specs=out_specs, check_vma=False)
```
